256 devices in a mesh: row: 4 (over y), col: 16 (over x, z_lo), depth: 4 (over z_hi, core).
Axes of the slice: x: 4, y: 4, z: 8 (z_hi: 2, z_lo: 4; z = z_hi * 4 + z_lo), core: 2. Of those that a mesh axis runs over, the one named last changes fastest.
Arguments:
- images: bfloat16 [4096, 1536], P(('row', 'col'), 'depth'), may hold values from -1.5 to 1.5
- texts: bfloat16 [24576, 1536], P(('row', 'col'), 'depth'), may hold values from -1.5 to 1.5
- image_potential: float32 [4096], P(('row', 'col')), may hold values from -1.75 to 0.75
- text_potential: float32 [24576], P(('row', 'col')), may hold values from -1.75 to 0.75
Outputs:
- grad_images: float32 [4096, 1536], P(('row', 'col'), 'depth')
- grad_texts: float32 [24576, 1536], P(('row', 'col'), 'depth')
The draws below stay inside these ranges and needn't reach their ends.
All inputs are finite; a program needn't handle non-finite values.
Results may differ from the reference program's by a relative error of at most 0.015.
Values may be sent and summed in bfloat16 or wider, within the bound.
A program may use at most 64 MiB of HBM per device.

```python
import jax
import jax.numpy as jnp
from jax import lax

WIDTH = 1536
IMAGES = 4096
TEXTS = 24576


def embed_draw(key, count):
    values = jnp.clip(jax.random.normal(key, (count, WIDTH), jnp.float32) * 0.25, -1.5, 1.5)
    return values.astype(jnp.bfloat16)


def draw_images(key, part):
    key = jax.random.fold_in(key, 11)
    return embed_draw(key, IMAGES)


def draw_texts(key, part):
    key = jax.random.fold_in(key, 12)
    return embed_draw(key, TEXTS)


def levels(stream_key, extent, pieces, low, largest):
    def one(axis_at, shards_of):
        heights = jax.random.uniform(jax.random.fold_in(jax.random.fold_in(stream_key, 6), axis_at), (shards_of,), jnp.float32, low / len(pieces), largest / len(pieces))
        return jnp.repeat(jnp.exp(heights), extent[axis_at] // shards_of).reshape((-1,) + (1,) * (len(extent) - axis_at - 1))

    level = one(*pieces[0])
    for cut in pieces[1:]:
        level = level * one(*cut)
    return level


def setup_inputs(seed: int = 0) -> dict:
    key_list = jax.random.split(jax.random.key(seed), 5)
    return {
        "images": draw_images(jax.random.fold_in(key_list[4], 71), 0),
        "texts": draw_texts(jax.random.fold_in(key_list[4], 71), 0),
        "image_potential": jnp.clip(-1.75 + 2.5 * jax.random.uniform(key_list[2], (IMAGES,), jnp.float32) ** levels(key_list[2], (IMAGES,), ((0, 64),), -0.2, 0.2), -1.75, 0.75),
        "text_potential": jnp.clip(-1.75 + 2.5 * jax.random.uniform(key_list[3], (TEXTS,), jnp.float32) ** levels(key_list[3], (TEXTS,), ((0, 64),), -0.2, 0.2), -1.75, 0.75),
    }


INV_TEMP = 0.4
LOSS_SCALE = 16.0


def reference(images, texts, image_potential, text_potential):
    block_rows = min(512, IMAGES)
    block_count = IMAGES // block_rows

    def one_block(total_grad, block_index):
        start = (block_index * block_rows).astype(jnp.int32)
        image_block = lax.dynamic_slice_in_dim(images, start, block_rows, 0)
        shift_block = lax.dynamic_slice_in_dim(image_potential, start, block_rows, 0)
        scores = jnp.dot(image_block, texts.T, preferred_element_type=jnp.float32)
        transport = jnp.exp(scores * INV_TEMP + shift_block[:, None] + text_potential[None, :]).astype(jnp.bfloat16)
        image_terms = jnp.dot(transport, texts, preferred_element_type=jnp.float32)
        total_grad = total_grad + jnp.dot(transport.T, image_block, preferred_element_type=jnp.float32)
        return total_grad, image_terms

    start_total = jnp.zeros((TEXTS, WIDTH), jnp.float32)
    text_total, image_terms = lax.scan(one_block, start_total, jnp.arange(block_count, dtype=jnp.int32))
    grad_images = image_terms.reshape(IMAGES, WIDTH) * (-LOSS_SCALE / TEXTS)
    grad_texts = text_total * (-LOSS_SCALE / IMAGES)
    return grad_images, grad_texts
```

```python
import functools

import jax
import jax.numpy as jnp
from jax import lax
from jax.experimental import pallas as pl
from jax.experimental.pallas import tpu as pltpu
from jax.sharding import PartitionSpec as P

INV_TEMP = 0.4
LOSS_SCALE = 16.0
MESH = pl.DeviceIdType.MESH
F32, BF16 = jnp.float32, jnp.bfloat16
ZORDER = (0, 1, 7, 2, 6, 3, 5, 4)
RING = (1, 3, 2)
W = 384


def dev(x, y, z, c):
    return (y, x * 4 + z % 4, (z // 4) * 2 + c)


def cols(q, n=W):
    return pl.ds(pl.multiple_of(q * W, W), n)


def kernel(
    img_in, txt_in, ip_in, tp_in, gi_out, gt_out,
    img, txt, plan, ap, aps, tp,
    gi_own, gi_send, gi_recv, gz_send, gz_recv,
    gt_own, gx_send, gx_recv, gy_send, gy_recv, gf_send, gf_recv,
    loc_sem, yn_s, yn_r, ye_s, ye_r, ex_s, ex_r, ch_s, ch_r, iz_s, iz_r, ix_s, ix_r,
    tp_s, tp_r, ap_s, ap_r, aps_s, aps_r,
    gi_s, gi_r, gz_s, gz_r, gx_s, gx_r, gy_s, gy_r, gf_s, gf_r,
):
    y = lax.axis_index("row")
    col = lax.axis_index("col")
    d = lax.axis_index("depth")
    x, zl, h, c = col // 4, col % 4, d // 2, d % 2
    z = h * 4 + zl
    o = 1 - c
    q = 2 * h + c

    def rc(src, dst, ss, rs, target):
        return pltpu.make_async_remote_copy(
            src_ref=src, dst_ref=dst, send_sem=ss, recv_sem=rs, device_id=target, device_id_type=MESH
        )

    me_o = dev(x, y, z, o)
    bar = pltpu.get_barrier_semaphore()
    partners = [me_o]
    partners += [dev((x + k) % 4, y, z, c) for k in RING]
    partners += [dev(x, (y + k) % 4, z, c) for k in RING]
    partners += [dev(x, y, (z + k) % 8, cc) for k in ZORDER[1:] for cc in (0, 1)]
    for p in partners:
        pl.semaphore_signal(bar, inc=1, device_id=p, device_id_type=MESH)
    aps[x] = ip_in[...]
    tp[y] = tp_in[...]
    pl.semaphore_wait(bar, len(partners))

    sends = []

    def go(cp):
        cp.start()
        sends.append(cp)

    mine = txt_in.at[pl.ds(h * 2, 2)]
    for k in RING:
        go(rc(mine, txt.at[:, y, :, cols(q)], yn_s.at[k], yn_r.at[y], dev(x, (y + k) % 4, z, c)))
    go(rc(txt_in.at[pl.ds((1 - h) * 2, 2)], txt.at[:, y, :, cols(q)], ex_s.at[0], ex_r.at[0], dev(x, y, (z + 4) % 8, c)))
    loc_t = pltpu.make_async_copy(mine, txt.at[:, y, :, cols(q)], loc_sem.at[0])
    loc_t.start()
    rows_here = pl.ds(pl.multiple_of(zl * 32, 32), 32)
    for j, k in enumerate(ZORDER[1:]):
        for r in (0, 1):
            go(rc(img_in.at[pl.ds(r * 32, 32)], img.at[x, rows_here, cols(q)], iz_s.at[2 * k + r],
                  iz_r.at[2 * z + c], dev(x, y, (z + k) % 8, r)))
    go(rc(img_in.at[pl.ds(pl.multiple_of(o * 32, 32), 32)], img.at[x, rows_here, cols(q)], iz_s.at[0],
          iz_r.at[2 * z + c], me_o))
    loc_i = pltpu.make_async_copy(
        img_in.at[pl.ds(pl.multiple_of(c * 32, 32), 32)], img.at[x, rows_here, cols(q)], loc_sem.at[1])
    loc_i.start()
    go(rc(mine, txt.at[:, y, :, cols(q)], ch_s.at[0], ch_r.at[2 * y + h], me_o))
    for k in RING:
        go(rc(tp.at[y], tp.at[y], tp_s.at[k], tp_r.at[y], dev(x, (y + k) % 4, z, c)))
        go(rc(aps.at[x], ap.at[zl], ap_s.at[k], ap_r.at[zl], dev(x, y, h * 4 + (zl + k) % 4, c)))
    loc_t.wait()
    loc_i.wait()

    def piece(xx, zz):
        return img.at[xx, pl.ds(pl.multiple_of((zz % 4) * 32, 32), 32), cols(2 * (zz // 4), 2 * W)]

    def wait_iz(zz, cc):
        dst = img.at[x, pl.ds(pl.multiple_of((zz % 4) * 32, 32), 32), cols(2 * (zz // 4) + cc)]
        rc(dst, dst, iz_s.at[0], iz_r.at[2 * zz + cc], me_o).wait_recv()

    def wait_txt(sem, yy, qq):
        dst = txt.at[:, yy, :, cols(qq)]
        rc(dst, dst, yn_s.at[0], sem, me_o).wait_recv()

    qp = 2 * (1 - h) + c
    for j, k in enumerate(ZORDER):
        zz = (z + k) % 8
        if k == 0:
            wait_iz(z, o)
        else:
            wait_iz(zz, 0)
            wait_iz(zz, 1)
        for kx in RING:
            go(rc(piece(x, zz), piece(x, zz), ix_s.at[8 * kx + k], ix_r.at[8 * x + zz], dev((x + kx) % 4, y, z, c)))
        if j == 2:
            for ky in RING[:2]:
                yy = (y + ky) % 4
                wait_txt(yn_r.at[yy], yy, q)
                go(rc(txt.at[:, yy, :, cols(q)], txt.at[:, yy, :, cols(q)], ch_s.at[2 * ky], ch_r.at[2 * yy + h], me_o))
        if j == 4:
            wait_txt(ex_r.at[0], y, qp)
            for ky in RING:
                go(rc(txt.at[:, y, :, cols(qp)], txt.at[:, y, :, cols(qp)], ye_s.at[ky], ye_r.at[y],
                      dev(x, (y + ky) % 4, z, c)))
            go(rc(txt.at[:, y, :, cols(qp)], txt.at[:, y, :, cols(qp)], ch_s.at[1], ch_r.at[2 * y + 1 - h], me_o))
            yy = (y + 2) % 4
            wait_txt(yn_r.at[yy], yy, q)
            go(rc(txt.at[:, yy, :, cols(q)], txt.at[:, yy, :, cols(q)], ch_s.at[4], ch_r.at[2 * yy + h], me_o))

    asum = aps[x]
    for k in RING:
        zz = (zl + k) % 4
        rc(ap.at[zz], ap.at[zz], ap_s.at[0], ap_r.at[zz], me_o).wait_recv()
        asum = asum + ap[zz]
    ap[zl] = asum
    for kx in RING:
        go(rc(ap.at[zl], aps.at[x], aps_s.at[kx], aps_r.at[x], dev((x + kx) % 4, y, z, c)))

    for ky in RING:
        yy = (y + ky) % 4
        wait_txt(ye_r.at[yy], yy, qp)
        go(rc(txt.at[:, yy, :, cols(qp)], txt.at[:, yy, :, cols(qp)], ch_s.at[2 * ky + 1], ch_r.at[2 * yy + 1 - h], me_o))
    tsum = tp[y]
    for ky in RING:
        yy = (y + ky) % 4
        rc(tp.at[yy], tp.at[yy], tp_s.at[0], tp_r.at[yy], me_o).wait_recv()
        tsum = tsum + tp[yy]
    b = tsum[0:1]
    for ky in (0,) + RING:
        yy = (y + ky) % 4
        wait_txt(ch_r.at[2 * yy + h], yy, 2 * h + o)
        wait_txt(ch_r.at[2 * yy + 1 - h], yy, 2 * (1 - h) + o)

    texts = txt[...].reshape(768, 4 * W)
    for i, k in enumerate((0,) + RING):
        xx = (x + k) % 4
        if k == 0:
            a = asum[0:1]
        else:
            for kz in ZORDER:
                zz = (z + kz) % 8
                rc(piece(xx, zz), piece(xx, zz), ix_s.at[0], ix_r.at[8 * xx + zz], me_o).wait_recv()
            rc(aps.at[xx], aps.at[xx], aps_s.at[0], aps_r.at[xx], me_o).wait_recv()
            a = aps[xx][0:1]
        a = jnp.broadcast_to(a, (128, 128)).T
        s = lax.dot_general(img[xx], texts, (((1,), (1,)), ((), ())), preferred_element_type=F32)
        p = jnp.exp(s * INV_TEMP + jnp.concatenate([a] * 6, axis=1) + b).astype(BF16)
        plan[xx] = p
        g = jnp.dot(p, texts, preferred_element_type=F32) * (-LOSS_SCALE / 24576)
        if k == 0:
            gi_own[...] = g
        else:
            gi_send[i - 1] = g.astype(BF16)
            for zz in range(4):
                part = pl.ds(zz * 32, 32)
                go(rc(gi_send.at[i - 1, part], gi_recv.at[k - 1, part], gi_s.at[4 * k + zz], gi_r.at[4 * k + zz],
                      dev(xx, y, z, c)))

    images = img[...].reshape(512, 4 * W)

    def text_terms(half):
        p = plan[:, :, pl.ds(pl.multiple_of(half * W, W), W)].reshape(512, W)
        return lax.dot_general(p, images, (((0,), (0,)), ((), ())), preferred_element_type=F32) * (-LOSS_SCALE / 4096)

    gx_send[...] = text_terms(o).astype(BF16)
    go(rc(gx_send, gx_recv, gx_s.at[0], gx_r.at[0], me_o))
    gt_own[...] = text_terms(c)
    rc(gx_recv, gx_recv, gx_s.at[0], gx_r.at[0], me_o).wait_recv()

    for j in (0, 1):
        hh = (1 - h) if j == 0 else h
        cc = cols(2 * hh, 2 * W)
        for i, k in enumerate(RING):
            yy = (y + k) % 4
            rows = pl.ds(pl.multiple_of(yy * 96, 96), 96)
            gy_send[j, i] = (gt_own[rows, cc] + gx_recv[rows, cc].astype(F32)).astype(BF16)
            go(rc(gy_send.at[j, i], gy_recv.at[j, k - 1], gy_s.at[4 * j + k], gy_r.at[4 * j + k], dev(x, yy, z, c)))

    for zz in range(4):
        part = pl.ds(zz * 32, 32)
        t = gi_own[part]
        for k in RING:
            rc(gi_recv.at[k - 1, part], gi_recv.at[k - 1, part], gi_s.at[0], gi_r.at[4 * k + zz], me_o).wait_recv()
            t = t + gi_recv[k - 1, part].astype(F32)
        t = t.astype(BF16)
        for qq in range(4):
            gz_send[zz * 4 + qq] = t[:, qq * W : (qq + 1) * W]
    for k in ZORDER[1:]:
        zz = (z + k) % 8
        for cc in (0, 1):
            go(rc(gz_send.at[(zz % 4) * 4 + (zz // 4) * 2 + cc], gz_recv.at[z, c], gz_s.at[2 * k + cc],
                  gz_r.at[2 * z + c], dev(x, y, zz, cc)))
    go(rc(gz_send.at[zl * 4 + h * 2 + o], gz_recv.at[z, c], gz_s.at[0], gz_r.at[2 * z + c], me_o))
    gz_recv[z, c] = gz_send[zl * 4 + q]

    mine_y = pl.ds(pl.multiple_of(y * 96, 96), 96)
    for j in (0, 1):
        hh = (1 - h) if j == 0 else h
        cc = cols(2 * hh, 2 * W)
        t = gt_own[mine_y, cc] + gx_recv[mine_y, cc].astype(F32)
        for k in RING:
            rc(gy_recv.at[j, k - 1], gy_recv.at[j, k - 1], gy_s.at[0], gy_r.at[4 * j + k], me_o).wait_recv()
            t = t + gy_recv[j, k - 1].astype(F32)
        for cc in (0, 1):
            gf_send[j, cc] = t[:, cc * W : (cc + 1) * W].astype(BF16)
        if j == 0:
            for cc in (0, 1):
                go(rc(gf_send.at[0, cc], gf_recv.at[h * 2 + c], gf_s.at[cc], gf_r.at[h * 2 + c],
                      dev(x, y, (z + 4) % 8, cc)))
        else:
            go(rc(gf_send.at[1, o], gf_recv.at[h * 2 + c], gf_s.at[2], gf_r.at[h * 2 + c], me_o))
            gf_recv[h * 2 + c] = gf_send[1, c]

    for k in ZORDER[1:]:
        zz = (z + k) % 8
        for cc in (0, 1):
            rc(gz_recv.at[zz, cc], gz_recv.at[zz, cc], gz_s.at[0], gz_r.at[2 * zz + cc], me_o).wait_recv()
    rc(gz_recv.at[z, o], gz_recv.at[z, o], gz_s.at[0], gz_r.at[2 * z + o], me_o).wait_recv()
    for r in (0, 1):
        t = gz_recv[0, r].astype(F32)
        for zz in range(1, 8):
            t = t + gz_recv[zz, r].astype(F32)
        gi_out[r * 32 : (r + 1) * 32] = t

    for dd in (h * 2 + o, (1 - h) * 2, (1 - h) * 2 + 1):
        rc(gf_recv.at[dd], gf_recv.at[dd], gf_s.at[0], gf_r.at[dd], me_o).wait_recv()
    for dd in range(4):
        gt_out[dd * 96 : (dd + 1) * 96] = gf_recv[dd].astype(F32)

    for cp in sends:
        cp.wait_send()


def on_device(images, texts, image_potential, text_potential):
    y = lax.axis_index("row")
    zl = lax.axis_index("col") % 4
    h, c = lax.axis_index("depth") // 2, lax.axis_index("depth") % 2
    lane = lax.iota(jnp.int32, 128) // 32
    half = lax.dynamic_slice(image_potential, (c * 32,), (32,))
    ip = jnp.where(lane == zl, jnp.tile(half, 4), 0.0)
    ip = jnp.broadcast_to(ip[None], (8, 128))
    th = lax.dynamic_slice(text_potential, (h * 192,), (192,)).reshape(2, 1, 96)
    tp = jnp.where((jnp.arange(4) == y)[None, :, None], th, 0.0).reshape(1, 768)
    tp = jnp.broadcast_to(tp, (8, 768))
    dma = pltpu.SemaphoreType.DMA
    vm = pltpu.VMEM
    return pl.pallas_call(
        kernel,
        out_shape=(jax.ShapeDtypeStruct((64, W), F32), jax.ShapeDtypeStruct((384, W), F32)),
        in_specs=[
            pl.BlockSpec(memory_space=pl.ANY),
            pl.BlockSpec(memory_space=pl.ANY),
            pl.BlockSpec(memory_space=pltpu.VMEM),
            pl.BlockSpec(memory_space=pltpu.VMEM),
        ],
        out_specs=(pl.BlockSpec(memory_space=pltpu.VMEM), pl.BlockSpec(memory_space=pltpu.VMEM)),
        scratch_shapes=[
            vm((4, 128, 4 * W), BF16), vm((2, 4, 96, 4 * W), BF16), vm((4, 128, 768), BF16),
            vm((4, 8, 128), F32), vm((4, 8, 128), F32), vm((4, 8, 768), F32),
            vm((128, 4 * W), F32), vm((3, 128, 4 * W), BF16), vm((3, 128, 4 * W), BF16),
            vm((16, 32, W), BF16), vm((8, 2, 32, W), BF16),
            vm((384, 4 * W), F32), vm((384, 4 * W), BF16), vm((384, 4 * W), BF16),
            vm((2, 3, 96, 2 * W), BF16), vm((2, 3, 96, 2 * W), BF16), vm((2, 2, 96, W), BF16), vm((4, 96, W), BF16),
            dma((2,)), dma((4,)), dma((4,)), dma((4,)), dma((4,)), dma((1,)), dma((1,)), dma((8,)), dma((8,)),
            dma((16,)), dma((16,)), dma((32,)), dma((32,)),
            dma((4,)), dma((4,)), dma((4,)), dma((4,)), dma((4,)), dma((4,)),
            dma((16,)), dma((16,)), dma((16,)), dma((16,)), dma((1,)), dma((1,)), dma((8,)), dma((8,)), dma((4,)), dma((4,)),
        ],
        compiler_params=pltpu.CompilerParams(
            collective_id=0, has_side_effects=True, vmem_limit_bytes=48 * 1024 * 1024
        ),
        cost_estimate=pl.CostEstimate(flops=3623878656, bytes_accessed=2000000, transcendentals=393216),
    )(images, texts.reshape(4, 96, W), ip, tp)


def solution(mesh):
    placed = (
        P(("row", "col"), "depth"),
        P(("row", "col"), "depth"),
        P(("row", "col")),
        P(("row", "col")),
    )
    return jax.shard_map(
        on_device,
        mesh=mesh,
        in_specs=placed,
        out_specs=(P(("row", "col"), "depth"), P(("row", "col"), "depth")),
        check_vma=False,
    )
```

```python
import jax
import jax.numpy as jnp
from jax import lax
from jax.experimental import pallas as pl
from jax.experimental.pallas import tpu as pltpu
from jax.sharding import PartitionSpec as P

INV_TEMP = 0.4
LOSS_SCALE = 16.0
MESH = pl.DeviceIdType.MESH
F32, BF16 = jnp.float32, jnp.bfloat16
ZORDER = (1, 7, 2, 6, 4)
RING = (1, 3, 2)
ORDER = (0, 1, 3, 2)
W = 384


def dev(x, y, z, c):
    return (y, x * 4 + z % 4, (z // 4) * 2 + c)


def cols(q, n=W):
    return pl.ds(pl.multiple_of(q * W, W), n)


def kernel(
    img_in, txt_in, ip_in, tp_in, gi_out, gt_out,
    img, txt, plan, ipv, tpv, ap, aps, tp,
    gi_own, gi_send, gi_recv, gz_send, gz, gf, gq_recv, gr_recv,
    gt_own, gx_send, gx_recv, gy_send, gy_recv, gf_send,
    loc_sem, yn_s, yn_r, ye_s, ye_r, ex_s, ex_r, ch_s, ch_r, iz_s, iz_r, ix_s, ix_r, fw_s, fw_r,
    tp_s, tp_r, ap_s, ap_r, aps_s, aps_r,
    gi_s, gi_r, gz_s, gz_r, gr_s, gr_r, gx_s, gx_r, gy_s, gy_r, gf_s, gf_r,
):
    y = lax.axis_index("row")
    col = lax.axis_index("col")
    d = lax.axis_index("depth")
    x, zl, h, c = col // 4, col % 4, d // 2, d % 2
    z = h * 4 + zl
    o = 1 - c
    q = 2 * h + c
    qp = 2 * (1 - h) + c

    def rc(src, dst, ss, rs, target):
        return pltpu.make_async_remote_copy(
            src_ref=src, dst_ref=dst, send_sem=ss, recv_sem=rs, device_id=target, device_id_type=MESH
        )

    me_o = dev(x, y, z, o)

    def got(dst, rs):
        rc(dst, dst, yn_s.at[0], rs, me_o).wait_recv()

    bar = pltpu.get_barrier_semaphore()
    partners = [me_o]
    partners += [dev((x + k) % 4, y, z, c) for k in RING]
    partners += [dev(x, (y + k) % 4, z, c) for k in RING]
    partners += [dev(x, y, (z + k) % 8, cc) for k in ZORDER for cc in (0, 1)]
    partners += [dev(x, y, (z + k) % 8, c) for k in (3, 5)]
    for p in partners:
        pl.semaphore_signal(bar, inc=1, device_id=p, device_id_type=MESH)

    lp = [pltpu.make_async_copy(ip_in, ipv, loc_sem.at[2]), pltpu.make_async_copy(tp_in, tpv, loc_sem.at[3])]
    for cp in lp:
        cp.start()
    for cp in lp:
        cp.wait()
    lane = lax.broadcasted_iota(jnp.int32, (8, 128), 1)
    v = ipv[...].reshape(1, 64)
    v = jnp.broadcast_to(jnp.concatenate([v, v], axis=1), (8, 128))
    v = pltpu.roll(v, ((zl + 4 - c) % 4) * 32, 1)
    aps[x] = jnp.where(lane // 32 == zl, v, 0.0)
    lane = lax.broadcasted_iota(jnp.int32, (8, W), 1)
    v = jnp.broadcast_to(tpv[...].reshape(1, W), (8, W))
    for s in (0, 1):
        t = pltpu.roll(v, (y * 96 + 2 * W - h * 192 - s * 96) % W, 1)
        tp[y, :, s * W : (s + 1) * W] = jnp.where(lane // 96 == y, t, 0.0)
    pl.semaphore_wait(bar, len(partners))

    sends = []

    def go(cp):
        cp.start()
        sends.append(cp)

    def text_piece(yy, qq, s):
        return txt.at[s, yy, :, cols(qq)]

    mine = txt_in.at[pl.ds(h * 2, 2)]
    rows_here = pl.ds(pl.multiple_of(x * 32, 32), 32)
    go(rc(img_in.at[pl.ds(pl.multiple_of(o * 32, 32), 32)], img.at[zl, rows_here, cols(q)], iz_s.at[0],
          iz_r.at[2 * z + c], me_o))
    for k in (1, 7, 2, 6):
        for r in (0, 1):
            go(rc(img_in.at[pl.ds(r * 32, 32)], img.at[zl, rows_here, cols(q)], iz_s.at[2 * min(k, 8 - k) + r + (8 if k > 4 else 0)],
                  iz_r.at[2 * z + c], dev(x, y, (z + k) % 8, r)))
    for k in RING:
        go(rc(mine, txt.at[:, y, :, cols(q)], yn_s.at[k], yn_r.at[y], dev(x, (y + k) % 4, z, c)))
    for s in (0, 1):
        go(rc(txt_in.at[(1 - h) * 2 + s], text_piece(y, q, s), ex_s.at[s], ex_r.at[s], dev(x, y, (z + 4) % 8, c)))
    loc_i = pltpu.make_async_copy(
        img_in.at[pl.ds(pl.multiple_of(c * 32, 32), 32)], img.at[zl, rows_here, cols(q)], loc_sem.at[1])
    loc_i.start()
    loc_t = pltpu.make_async_copy(mine, txt.at[:, y, :, cols(q)], loc_sem.at[0])
    loc_t.start()
    go(rc(mine, txt.at[:, y, :, cols(q)], ch_s.at[0], ch_r.at[y], me_o))
    for k in RING:
        go(rc(tp.at[y], tp.at[y], tp_s.at[k], tp_r.at[y], dev(x, (y + k) % 4, z, c)))
        go(rc(aps.at[x], ap.at[zl], ap_s.at[k], ap_r.at[zl], dev(x, y, h * 4 + (zl + k) % 4, c)))
    loc_i.wait()

    def piece(xx, zz, start=0, n=32):
        return img.at[zz % 4, pl.ds(pl.multiple_of(xx * 32 + start, 16), n), cols(2 * (zz // 4), 2 * W)]

    def pass_on(k):
        zz = (z + k) % 8
        for e, kx in ((0, 1), (1, 3)):
            back = (x + 4 - kx) % 4
            got(piece(back, zz), ix_r.at[8 * back + zz])
            half = piece(back, zz, 16 * e, 16)
            go(rc(half, half, fw_s.at[2 * k + e], fw_r.at[2 * zz + e], dev((x + kx) % 4, y, z, c)))

    def along_x(k):
        zz = (z + k) % 8
        if k == 0:
            got(img.at[zl, rows_here, cols(2 * h + o)], iz_r.at[2 * z + o])
        elif k in (3, 5):
            got(piece(x, zz), iz_r.at[2 * zz])
        elif k == 4:
            for e in (0, 1):
                got(piece(x, zz, 16 * e, 16), iz_r.at[2 * zz + e])
        else:
            for cc in (0, 1):
                got(img.at[zz % 4, rows_here, cols(2 * (zz // 4) + cc)], iz_r.at[2 * zz + cc])
        if k in (2, 6):
            e, step = (1, 7) if k == 2 else (0, 1)
            p = piece(x, zz)
            go(rc(p, p, iz_s.at[6 + 2 * e], iz_r.at[2 * zz], dev(x, y, (z + step) % 8, c)))
            p = piece(x, zz, 16 * e, 16)
            go(rc(p, p, iz_s.at[7 + 2 * e], iz_r.at[2 * zz + e], dev(x, y, (z + 2 * step) % 8, c)))
        for e, kx in ((0, 1), (1, 3)):
            go(rc(piece(x, zz), piece(x, zz), ix_s.at[2 * k + e], ix_r.at[8 * x + zz], dev((x + kx) % 4, y, z, c)))

    def forward_swapped(s):
        p = text_piece(y, qp, s)
        got(p, ex_r.at[s])
        for ky in RING:
            go(rc(p, p, ye_s.at[2 * ky + s], ye_r.at[2 * y + s], dev(x, (y + ky) % 4, z, c)))
        go(rc(p, p, ch_s.at[4 + s], ch_r.at[4 + 2 * y + s], me_o))

    def to_other_core(ky):
        yy = (y + ky) % 4
        p = txt.at[:, yy, :, cols(q)]
        got(p, yn_r.at[yy])
        go(rc(p, p, ch_s.at[ky], ch_r.at[yy], me_o))

    along_x(0)
    along_x(1)
    along_x(7)
    pass_on(0)
    along_x(2)
    along_x(6)
    forward_swapped(0)
    pass_on(1)
    pass_on(7)
    along_x(3)
    along_x(5)
    forward_swapped(1)
    pass_on(2)
    pass_on(6)
    along_x(4)
    for k in RING:
        to_other_core(k)
    pass_on(3)
    pass_on(5)
    pass_on(4)

    asum = aps[x]
    for k in RING:
        zz = (zl + k) % 4
        got(ap.at[zz], ap_r.at[zz])
        asum = asum + ap[zz]
    ap[zl] = asum
    for kx in RING:
        go(rc(ap.at[zl], aps.at[x], aps_s.at[kx], aps_r.at[x], dev((x + kx) % 4, y, z, c)))

    for s in (0, 1):
        for ky in RING:
            yy = (y + ky) % 4
            p = text_piece(yy, qp, s)
            got(p, ye_r.at[2 * yy + s])
            go(rc(p, p, ch_s.at[4 + 2 * ky + s], ch_r.at[4 + 2 * yy + s], me_o))
    loc_t.wait()
    tsum = tp[y]
    for ky in RING:
        yy = (y + ky) % 4
        got(tp.at[yy], tp_r.at[yy])
        tsum = tsum + tp[yy]
    b = tsum[0:1]
    a_of = {0: jnp.broadcast_to(asum[0:1], (128, 128)).T}
    for kx in RING:
        xx = (x + kx) % 4
        got(aps.at[xx], aps_r.at[xx])
        a_of[kx] = jnp.broadcast_to(aps[xx][0:1], (128, 128)).T
    for kx in (0,) + RING:
        gi_own[0, pl.ds(pl.multiple_of(((x + kx) % 4) * 128, 128), 128), 0:128] = a_of[kx]
    for ky in (0,) + RING:
        yy = (y + ky) % 4
        got(txt.at[:, yy, :, cols(2 * h + o)], ch_r.at[yy])
        for s in (0, 1):
            got(text_piece(yy, 2 * (1 - h) + o, s), ch_r.at[4 + 2 * yy + s])

    texts = txt[...].reshape(768, 4 * W)
    for zz in range(8):
        for e in (0, 1):
            got(piece((x + 2) % 4, zz, 16 * e, 16), fw_r.at[2 * zz + e])
    for half in (0, 1):
        a = jnp.concatenate(
            [gi_own[0, pl.ds(xx * 128 + zz * 32, 32), 0:128] for zz in (2 * half, 2 * half + 1) for xx in range(4)], axis=0)
        i = img[2 * half : 2 * half + 2].reshape(256, 4 * W)
        s = lax.dot_general(i, texts, (((1,), (1,)), ((), ())), preferred_element_type=F32)
        p = jnp.exp(s * INV_TEMP + jnp.concatenate([a] * 6, axis=1) + b).astype(BF16)
        plan[2 * half : 2 * half + 2] = p.reshape(2, 128, 768)

    def own_rows(j, k, e, n=16):
        return pl.ds(pl.multiple_of(j * 128 + ((x + k) % 4) * 32 + 16 * e, 16), n)

    def image_send(j, slot, kx):
        go(rc(gi_send.at[j, slot], gi_recv.at[j, slot], gi_s.at[6 * j + slot], gi_r.at[6 * j + slot],
              dev((x + kx) % 4, y, z, c)))

    def image_terms(j):
        zj = (zl + ORDER[j]) % 4
        gi_own[1, pl.ds(j * 128, 128)] = jnp.dot(plan[zj], texts, preferred_element_type=F32) * (-LOSS_SCALE / 24576)
        for slot, (k, e, kx) in enumerate(((2, 0, 1), (2, 1, 3), (1, 1, 1), (3, 0, 3))):
            gi_send[j, slot] = gi_own[1, own_rows(j, k, e)].astype(BF16)
            image_send(j, slot, kx)

    def image_relay(j):
        for slot, (k, e) in enumerate(((1, 0), (3, 1))):
            got(gi_recv.at[j, slot], gi_r.at[6 * j + slot])
            gi_send[j, 4 + slot] = (gi_own[1, own_rows(j, k, e)] + gi_recv[j, slot].astype(F32)).astype(BF16)
            image_send(j, 4 + slot, k)

    def text_terms(half, cc):
        p = plan[:, :, pl.ds(pl.multiple_of(half * W, W), W)].reshape(512, W)
        i = img[:, :, cc].reshape(512, 2 * W)
        return lax.dot_general(p, i, (((0,), (0,)), ((), ())), preferred_element_type=F32) * (-LOSS_SCALE / 4096)

    wide = [cols(2 * (1 - h), 2 * W), cols(2 * h, 2 * W)]

    def text_other(j):
        gx_send[j] = text_terms(o, wide[j]).astype(BF16)
        go(rc(gx_send.at[j], gx_recv.at[j], gx_s.at[j], gx_r.at[j], me_o))

    def text_own(j):
        gt_own[j] = text_terms(c, wide[j])
        got(gx_recv.at[j], gx_r.at[j])
        for i, k in enumerate(RING):
            yy = (y + k) % 4
            rows = pl.ds(pl.multiple_of(yy * 96, 96), 96)
            gy_send[j, i] = (gt_own[j, rows] + gx_recv[j, rows].astype(F32)).astype(BF16)
            go(rc(gy_send.at[j, i], gy_recv.at[j, k - 1], gy_s.at[4 * j + k], gy_r.at[4 * j + k], dev(x, yy, z, c)))

    def image_sums(j):
        for slot in (2, 3, 4, 5):
            got(gi_recv.at[j, slot], gi_r.at[6 * j + slot])
        for e, slots in ((0, (3, 4)), (1, (2, 5))):
            t = gi_own[1, own_rows(j, 0, e)]
            for slot in slots:
                t = t + gi_recv[j, slot].astype(F32)
            if j < 3:
                gz_send[j, 16 * e : 16 * e + 16] = t.astype(BF16)
            else:
                gi_own[0, 16 * e : 16 * e + 16] = t
        for dz in ((0, 4), (1, 5), (7, 3), (2, 6))[j]:
            zz = (z + dz) % 8
            both = cols(2 * (zz // 4), 2 * W)
            if dz == 4:
                for e, step in ((0, 2), (1, 6)):
                    go(rc(gz_send.at[j, pl.ds(16 * e, 16), both], gq_recv.at[e], gr_s.at[e], gr_r.at[e],
                          dev(x, y, (z + step) % 8, c)))
            elif dz in (3, 5):
                e, step = (0, 1) if dz == 3 else (1, 7)
                go(rc(gz_send.at[j, :, both], gr_recv.at[e], gr_s.at[2 + e], gr_r.at[2 + e],
                      dev(x, y, (z + step) % 8, c)))
            elif dz == 0:
                go(rc(gz_send.at[0, :, cols(2 * h + o)], gz.at[z, c], gz_s.at[0], gz_r.at[2 * z + c], me_o))
                gz[z, c] = gz_send[0, :, cols(q)]
            else:
                if dz in (2, 6):
                    e = 0 if dz == 2 else 1
                    got(gq_recv.at[e], gr_r.at[e])
                    got(gr_recv.at[e], gr_r.at[2 + e])
                    for g in (0, 1):
                        t = gi_own[0, 16 * g : 16 * g + 16, both] + gr_recv[e, 16 * g : 16 * g + 16].astype(F32)
                        if g == e:
                            t = t + gq_recv[e].astype(F32)
                        gz_send[j, 16 * g : 16 * g + 16, both] = t.astype(BF16)
                for cc in (0, 1):
                    go(rc(gz_send.at[j, :, cols(2 * (zz // 4) + cc)], gz.at[z, c], gz_s.at[2 * dz + cc],
                          gz_r.at[2 * z + c], dev(x, y, zz, cc)))

    def text_sums(j):
        mine_y = pl.ds(pl.multiple_of(y * 96, 96), 96)
        t = gt_own[j, mine_y] + gx_recv[j, mine_y].astype(F32)
        for k in RING:
            got(gy_recv.at[j, k - 1], gy_r.at[4 * j + k])
            t = t + gy_recv[j, k - 1].astype(F32)
        gf_send[j] = t.astype(BF16)
        part = gf.at[h * 2 + c]
        if j == 0:
            for cc in (0, 1):
                go(rc(gf_send.at[0, :, pl.ds(cc * W, W)], part, gf_s.at[cc], gf_r.at[h * 2 + c], dev(x, y, (z + 4) % 8, cc)))
        else:
            go(rc(gf_send.at[1, :, cols(o)], part, gf_s.at[2], gf_r.at[h * 2 + c], me_o))
            gf[h * 2 + c] = gf_send[1, :, cols(c)]

    image_terms(0)
    text_other(0)
    image_terms(1)
    text_own(0)
    image_terms(2)
    text_other(1)
    image_terms(3)
    text_own(1)
    image_relay(0)
    image_relay(1)
    image_relay(2)
    image_relay(3)
    image_sums(0)
    image_sums(1)
    text_sums(0)
    image_sums(2)
    image_sums(3)
    text_sums(1)

    for k in (1, 7, 2, 6):
        zz = (z + k) % 8
        for cc in (0, 1):
            got(gz.at[zz, cc], gz_r.at[2 * zz + cc])
    got(gz.at[z, o], gz_r.at[2 * z + o])
    for dd in (h * 2 + o, (1 - h) * 2, (1 - h) * 2 + 1):
        got(gf.at[dd], gf_r.at[dd])
    for r in (0, 1):
        t = gz[z, r].astype(F32)
        for k in (1, 7, 2, 6):
            t = t + gz[(z + k) % 8, r].astype(F32)
        gi_out[r * 32 : (r + 1) * 32] = t
    for dd in range(4):
        gt_out[dd * 96 : (dd + 1) * 96] = gf[dd].astype(F32)
    for cp in sends:
        cp.wait_send()


def on_device(images, texts, image_potential, text_potential):
    dma = pltpu.SemaphoreType.DMA
    vm = pltpu.VMEM
    hbm = pl.BlockSpec(memory_space=pltpu.HBM)
    return pl.pallas_call(
        kernel,
        out_shape=(jax.ShapeDtypeStruct((64, W), F32), jax.ShapeDtypeStruct((384, W), F32)),
        in_specs=[hbm] * 4,
        out_specs=(pl.BlockSpec(memory_space=pltpu.VMEM), pl.BlockSpec(memory_space=pltpu.VMEM)),
        scratch_shapes=[
            vm((4, 128, 4 * W), BF16), vm((2, 4, 96, 4 * W), BF16), vm((4, 128, 768), BF16),
            vm((64,), F32), vm((W,), F32), vm((4, 8, 128), F32), vm((4, 8, 128), F32), vm((4, 8, 768), F32),
            vm((2, 512, 4 * W), F32), vm((4, 6, 16, 4 * W), BF16), vm((4, 6, 16, 4 * W), BF16), vm((4, 32, 4 * W), BF16),
            vm((8, 2, 32, W), BF16), vm((4, 96, W), BF16),
            vm((2, 16, 2 * W), BF16), vm((2, 32, 2 * W), BF16),
            vm((2, 384, 2 * W), F32), vm((2, 384, 2 * W), BF16), vm((2, 384, 2 * W), BF16),
            vm((2, 3, 96, 2 * W), BF16), vm((2, 3, 96, 2 * W), BF16), vm((2, 96, 2 * W), BF16),
            dma((4,)), dma((4,)), dma((4,)), dma((8,)), dma((8,)), dma((2,)), dma((2,)), dma((12,)), dma((12,)),
            dma((16,)), dma((16,)), dma((16,)), dma((32,)), dma((16,)), dma((16,)),
            dma((4,)), dma((4,)), dma((4,)), dma((4,)), dma((4,)), dma((4,)),
            dma((24,)), dma((24,)), dma((16,)), dma((16,)), dma((4,)), dma((4,)), dma((2,)), dma((2,)), dma((8,)), dma((8,)), dma((4,)), dma((4,)),
        ],
        compiler_params=pltpu.CompilerParams(
            collective_id=0, has_side_effects=True, vmem_limit_bytes=63 * 1024 * 1024
        ),
        cost_estimate=pl.CostEstimate(flops=3623878656, bytes_accessed=2000000, transcendentals=393216),
    )(images, texts.reshape(4, 96, W), image_potential, text_potential)


def solution(mesh):
    placed = (
        P(("row", "col"), "depth"),
        P(("row", "col"), "depth"),
        P(("row", "col")),
        P(("row", "col")),
    )
    return jax.shard_map(
        on_device,
        mesh=mesh,
        in_specs=placed,
        out_specs=(P(("row", "col"), "depth"), P(("row", "col"), "depth")),
        check_vma=False,
    )
```

```python
import jax
import jax.numpy as jnp
from jax import lax
from jax.experimental import pallas as pl
from jax.experimental.pallas import tpu as pltpu
from jax.sharding import PartitionSpec as P

INV_TEMP = 0.4
LOSS_SCALE = 16.0
MESH = pl.DeviceIdType.MESH
F32, BF16 = jnp.float32, jnp.bfloat16
ZORDER = (1, 7, 2, 6, 4)
RING = (1, 3, 2)
ORDER = (0, 1, 3, 2)
PAIRS = ((0, 4), (1, 5), (7, 3), (2, 6))
W = 384


def dev(x, y, z, c):
    return (y, x * 4 + z % 4, (z // 4) * 2 + c)


def cols(q, n=W):
    return pl.ds(pl.multiple_of(q * W, W), n)


def kernel(
    img_in, txt_in, ip_in, tp_in, gi_out, gt_out,
    img, txt, plan, ipv, tpv, ap, aps, tp,
    gi_own, gi_send, gi_recv, gz_send, gz, gf, gq_recv, gr_recv,
    gt_own, gx_send, gx_recv, gy_send, gy_recv, gf_send,
    loc_sem, yn_s, yn_r, ye_s, ye_r, ex_s, ex_r, ch_s, ch_r, iz_s, iz_r, ix_s, ix_r, fw_s, fw_r,
    tp_s, tp_r, ap_s, ap_r, aps_s, aps_r,
    gi_s, gi_r, gz_s, gz_r, gr_s, gr_r, gx_s, gx_r, gy_s, gy_r, gf_s, gf_r,
):
    y = lax.axis_index("row")
    col = lax.axis_index("col")
    d = lax.axis_index("depth")
    x, zl, h, c = col // 4, col % 4, d // 2, d % 2
    z = h * 4 + zl
    o = 1 - c
    q = 2 * h + c
    qp = 2 * (1 - h) + c

    def rc(src, dst, ss, rs, target):
        return pltpu.make_async_remote_copy(
            src_ref=src, dst_ref=dst, send_sem=ss, recv_sem=rs, device_id=target, device_id_type=MESH
        )

    me_o = dev(x, y, z, o)

    def got(dst, rs):
        rc(dst, dst, yn_s.at[0], rs, me_o).wait_recv()

    bar = pltpu.get_barrier_semaphore()
    partners = [me_o]
    partners += [dev((x + k) % 4, y, z, c) for k in RING]
    partners += [dev(x, (y + k) % 4, z, c) for k in RING]
    partners += [dev(x, y, (z + k) % 8, cc) for k in ZORDER for cc in (0, 1)]
    partners += [dev(x, y, (z + k) % 8, c) for k in (3, 5)]
    for p in partners:
        pl.semaphore_signal(bar, inc=1, device_id=p, device_id_type=MESH)

    lp = [pltpu.make_async_copy(ip_in, ipv, loc_sem.at[2]), pltpu.make_async_copy(tp_in, tpv, loc_sem.at[3])]
    for cp in lp:
        cp.start()
    for cp in lp:
        cp.wait()
    lane = lax.broadcasted_iota(jnp.int32, (8, 128), 1)
    v = ipv[...].reshape(1, 64)
    v = jnp.broadcast_to(jnp.concatenate([v, v], axis=1), (8, 128))
    v = pltpu.roll(v, ((zl + 4 - c) % 4) * 32, 1)
    aps[x] = jnp.where(lane // 32 == zl, v, 0.0)
    lane = lax.broadcasted_iota(jnp.int32, (8, W), 1)
    v = jnp.broadcast_to(tpv[...].reshape(1, W), (8, W))
    for s in (0, 1):
        t = pltpu.roll(v, (y * 96 + 2 * W - h * 192 - s * 96) % W, 1)
        tp[y, :, s * W : (s + 1) * W] = jnp.where(lane // 96 == y, t, 0.0)
    pl.semaphore_wait(bar, len(partners))

    sends = []

    def go(cp):
        cp.start()
        sends.append(cp)

    def text_piece(yy, qq, s):
        return txt.at[s, yy, :, cols(qq)]

    mine = txt_in.at[pl.ds(h * 2, 2)]
    rows_here = pl.ds(pl.multiple_of(x * 32, 32), 32)
    mine = txt_in.at[pl.ds(h * 2, 2)]

    def send_images(k):
        for r in (0, 1):
            go(rc(img_in.at[pl.ds(r * 32, 32)], img.at[zl, rows_here, cols(q)], iz_s.at[2 * min(k, 8 - k) + r + (8 if k > 4 else 0)],
                  iz_r.at[2 * z + c], dev(x, y, (z + k) % 8, r)))

    def send_texts():
        for k in RING:
            go(rc(mine, txt.at[:, y, :, cols(q)], yn_s.at[k], yn_r.at[y], dev(x, (y + k) % 4, z, c)))

    def swap_texts(s):
        go(rc(txt_in.at[(1 - h) * 2 + s], text_piece(y, q, s), ex_s.at[s], ex_r.at[s], dev(x, y, (z + 4) % 8, c)))

    go(rc(img_in.at[pl.ds(pl.multiple_of(o * 32, 32), 32)], img.at[zl, rows_here, cols(q)], iz_s.at[0],
          iz_r.at[2 * z + c], me_o))
    send_images(1)
    send_images(7)
    send_texts()
    swap_texts(0)
    send_images(2)
    send_images(6)
    swap_texts(1)
    loc_i = pltpu.make_async_copy(
        img_in.at[pl.ds(pl.multiple_of(c * 32, 32), 32)], img.at[zl, rows_here, cols(q)], loc_sem.at[1])
    loc_i.start()
    loc_t = pltpu.make_async_copy(mine, txt.at[:, y, :, cols(q)], loc_sem.at[0])
    loc_t.start()
    go(rc(mine, txt.at[:, y, :, cols(q)], ch_s.at[0], ch_r.at[y], me_o))
    for k in RING:
        go(rc(tp.at[y], tp.at[y], tp_s.at[k], tp_r.at[y], dev(x, (y + k) % 4, z, c)))
        go(rc(aps.at[x], ap.at[zl], ap_s.at[k], ap_r.at[zl], dev(x, y, h * 4 + (zl + k) % 4, c)))
    loc_i.wait()

    def piece(xx, zz, start=0, n=32):
        return img.at[zz % 4, pl.ds(pl.multiple_of(xx * 32 + start, 16), n), cols(2 * (zz // 4), 2 * W)]

    def pass_on(k):
        zz = (z + k) % 8
        for e, kx in ((0, 1), (1, 3)):
            back = (x + 4 - kx) % 4
            got(piece(back, zz), ix_r.at[8 * back + zz])
            half = piece(back, zz, 16 * e, 16)
            go(rc(half, half, fw_s.at[2 * k + e], fw_r.at[2 * zz + e], dev((x + kx) % 4, y, z, c)))

    def along_x(k):
        zz = (z + k) % 8
        if k == 0:
            got(img.at[zl, rows_here, cols(2 * h + o)], iz_r.at[2 * z + o])
        elif k in (3, 5):
            got(piece(x, zz), iz_r.at[2 * zz])
        elif k == 4:
            for e in (0, 1):
                got(piece(x, zz, 16 * e, 16), iz_r.at[2 * zz + e])
        else:
            for cc in (0, 1):
                got(img.at[zz % 4, rows_here, cols(2 * (zz // 4) + cc)], iz_r.at[2 * zz + cc])
        if k in (2, 6):
            e, step = (1, 7) if k == 2 else (0, 1)
            p = piece(x, zz)
            go(rc(p, p, iz_s.at[6 + 2 * e], iz_r.at[2 * zz], dev(x, y, (z + step) % 8, c)))
            p = piece(x, zz, 16 * e, 16)
            go(rc(p, p, iz_s.at[7 + 2 * e], iz_r.at[2 * zz + e], dev(x, y, (z + 2 * step) % 8, c)))
        for e, kx in ((0, 1), (1, 3)):
            go(rc(piece(x, zz), piece(x, zz), ix_s.at[2 * k + e], ix_r.at[8 * x + zz], dev((x + kx) % 4, y, z, c)))

    def forward_swapped(s):
        p = text_piece(y, qp, s)
        got(p, ex_r.at[s])
        for ky in RING:
            go(rc(p, p, ye_s.at[2 * ky + s], ye_r.at[2 * y + s], dev(x, (y + ky) % 4, z, c)))
        go(rc(p, p, ch_s.at[4 + s], ch_r.at[4 + 2 * y + s], me_o))

    def to_other_core(ky):
        yy = (y + ky) % 4
        p = txt.at[:, yy, :, cols(q)]
        got(p, yn_r.at[yy])
        go(rc(p, p, ch_s.at[ky], ch_r.at[yy], me_o))

    def swapped_to_other_core(s):
        for ky in RING:
            yy = (y + ky) % 4
            p = text_piece(yy, qp, s)
            got(p, ye_r.at[2 * yy + s])
            go(rc(p, p, ch_s.at[4 + 2 * ky + s], ch_r.at[4 + 2 * yy + s], me_o))

    along_x(0)
    along_x(1)
    along_x(7)
    pass_on(0)
    forward_swapped(0)
    along_x(2)
    along_x(6)
    pass_on(1)
    pass_on(7)
    forward_swapped(1)
    along_x(3)
    along_x(5)
    pass_on(2)
    pass_on(6)
    along_x(4)
    to_other_core(1)
    to_other_core(3)
    to_other_core(2)
    pass_on(3)
    pass_on(5)
    pass_on(4)
    swapped_to_other_core(0)
    swapped_to_other_core(1)

    asum = aps[x]
    for k in RING:
        zz = (zl + k) % 4
        got(ap.at[zz], ap_r.at[zz])
        asum = asum + ap[zz]
    ap[zl] = asum
    for kx in RING:
        go(rc(ap.at[zl], aps.at[x], aps_s.at[kx], aps_r.at[x], dev((x + kx) % 4, y, z, c)))

    loc_t.wait()
    tsum = tp[y]
    for ky in RING:
        yy = (y + ky) % 4
        got(tp.at[yy], tp_r.at[yy])
        tsum = tsum + tp[yy]
    b = tsum[0:1]
    a_of = {0: jnp.broadcast_to(asum[0:1], (128, 128)).T}
    for kx in RING:
        xx = (x + kx) % 4
        got(aps.at[xx], aps_r.at[xx])
        a_of[kx] = jnp.broadcast_to(aps[xx][0:1], (128, 128)).T
    for kx in (0,) + RING:
        gi_own[0, pl.ds(pl.multiple_of(((x + kx) % 4) * 128, 128), 128), 0:128] = a_of[kx]
    for ky in (0,) + RING:
        yy = (y + ky) % 4
        got(txt.at[:, yy, :, cols(2 * h + o)], ch_r.at[yy])
        for s in (0, 1):
            got(text_piece(yy, 2 * (1 - h) + o, s), ch_r.at[4 + 2 * yy + s])

    texts = txt[...].reshape(768, 4 * W)

    def scores(half):
        if half == 0:
            for zz in range(8):
                for e in (0, 1):
                    got(piece((x + 2) % 4, zz, 16 * e, 16), fw_r.at[2 * zz + e])
        a = jnp.concatenate(
            [gi_own[0, pl.ds(xx * 128 + zz * 32, 32), 0:128] for zz in (2 * half, 2 * half + 1) for xx in range(4)], axis=0)
        i = img[2 * half : 2 * half + 2].reshape(256, 4 * W)
        t = lax.dot_general(i, texts, (((1,), (1,)), ((), ())), preferred_element_type=F32)
        p = jnp.exp(t * INV_TEMP + jnp.concatenate([a] * 6, axis=1) + b).astype(BF16)
        plan[2 * half : 2 * half + 2] = p.reshape(2, 128, 768)

    def own_rows(j, k, e, n=16):
        return pl.ds(pl.multiple_of(j * 128 + ((x + k) % 4) * 32 + 16 * e, 16), n)

    def image_send(j, slot, kx):
        go(rc(gi_send.at[j, slot], gi_recv.at[j, slot], gi_s.at[6 * j + slot], gi_r.at[6 * j + slot],
              dev((x + kx) % 4, y, z, c)))

    def image_terms(j):
        zj = (zl + ORDER[j]) % 4
        gi_own[1, pl.ds(j * 128, 128)] = jnp.dot(plan[zj], texts, preferred_element_type=F32) * (-LOSS_SCALE / 24576)
        for slot, (k, e, kx) in enumerate(((2, 0, 1), (2, 1, 3), (1, 1, 1), (3, 0, 3))):
            gi_send[j, slot] = gi_own[1, own_rows(j, k, e)].astype(BF16)
            image_send(j, slot, kx)

    def image_relay(j):
        for slot, (k, e) in enumerate(((1, 0), (3, 1))):
            got(gi_recv.at[j, slot], gi_r.at[6 * j + slot])
            gi_send[j, 4 + slot] = (gi_own[1, own_rows(j, k, e)] + gi_recv[j, slot].astype(F32)).astype(BF16)
            image_send(j, 4 + slot, k)

    def text_terms(half, cc):
        p = plan[:, :, pl.ds(pl.multiple_of(half * W, W), W)].reshape(512, W)
        i = img[:, :, cc].reshape(512, 2 * W)
        return lax.dot_general(p, i, (((0,), (0,)), ((), ())), preferred_element_type=F32) * (-LOSS_SCALE / 4096)

    wide = [cols(2 * (1 - h), 2 * W), cols(2 * h, 2 * W)]

    def text_other(j):
        gx_send[j] = text_terms(o, wide[j]).astype(BF16)
        go(rc(gx_send.at[j], gx_recv.at[j], gx_s.at[j], gx_r.at[j], me_o))

    def text_own(j):
        gt_own[j] = text_terms(c, wide[j])
        got(gx_recv.at[j], gx_r.at[j])
        for i, k in enumerate(RING):
            yy = (y + k) % 4
            rows = pl.ds(pl.multiple_of(yy * 96, 96), 96)
            gy_send[j, i] = (gt_own[j, rows] + gx_recv[j, rows].astype(F32)).astype(BF16)
            go(rc(gy_send.at[j, i], gy_recv.at[j, k - 1], gy_s.at[4 * j + k], gy_r.at[4 * j + k], dev(x, yy, z, c)))

    def image_sums(j):
        for slot in (2, 3, 4, 5):
            got(gi_recv.at[j, slot], gi_r.at[6 * j + slot])
        for e, slots in ((0, (3, 4)), (1, (2, 5))):
            t = gi_own[1, own_rows(j, 0, e)]
            for slot in slots:
                t = t + gi_recv[j, slot].astype(F32)
            if j < 3:
                gz_send[j, 16 * e : 16 * e + 16] = t.astype(BF16)
            else:
                gi_own[0, 16 * e : 16 * e + 16] = t
        for dz in PAIRS[j]:
            zz = (z + dz) % 8
            both = cols(2 * (zz // 4), 2 * W)
            if dz == 4:
                for e, step in ((0, 2), (1, 6)):
                    go(rc(gz_send.at[j, pl.ds(16 * e, 16), both], gq_recv.at[e], gr_s.at[e], gr_r.at[e],
                          dev(x, y, (z + step) % 8, c)))
            elif dz in (3, 5):
                e, step = (0, 1) if dz == 3 else (1, 7)
                go(rc(gz_send.at[j, :, both], gr_recv.at[e], gr_s.at[2 + e], gr_r.at[2 + e],
                      dev(x, y, (z + step) % 8, c)))
            elif dz == 0:
                go(rc(gz_send.at[0, :, cols(2 * h + o)], gz.at[z, c], gz_s.at[0], gz_r.at[2 * z + c], me_o))
                gz[z, c] = gz_send[0, :, cols(q)]
            else:
                if dz in (2, 6):
                    e = 0 if dz == 2 else 1
                    got(gq_recv.at[e], gr_r.at[e])
                    got(gr_recv.at[e], gr_r.at[2 + e])
                    for g in (0, 1):
                        t = gi_own[0, 16 * g : 16 * g + 16, both] + gr_recv[e, 16 * g : 16 * g + 16].astype(F32)
                        if g == e:
                            t = t + gq_recv[e].astype(F32)
                        gz_send[j, 16 * g : 16 * g + 16, both] = t.astype(BF16)
                for cc in (0, 1):
                    go(rc(gz_send.at[j, :, cols(2 * (zz // 4) + cc)], gz.at[z, c], gz_s.at[2 * dz + cc],
                          gz_r.at[2 * z + c], dev(x, y, zz, cc)))

    def text_sums(j):
        mine_y = pl.ds(pl.multiple_of(y * 96, 96), 96)
        t = gt_own[j, mine_y] + gx_recv[j, mine_y].astype(F32)
        for k in RING:
            got(gy_recv.at[j, k - 1], gy_r.at[4 * j + k])
            t = t + gy_recv[j, k - 1].astype(F32)
        gf_send[j] = t.astype(BF16)
        part = gf.at[h * 2 + c]
        if j == 0:
            for cc in (0, 1):
                go(rc(gf_send.at[0, :, pl.ds(cc * W, W)], part, gf_s.at[cc], gf_r.at[h * 2 + c], dev(x, y, (z + 4) % 8, cc)))
        else:
            go(rc(gf_send.at[1, :, cols(o)], part, gf_s.at[2], gf_r.at[h * 2 + c], me_o))
            gf[h * 2 + c] = gf_send[1, :, cols(c)]

    scores(0)
    scores(1)
    text_other(0)
    image_terms(0)
    text_own(0)
    image_terms(1)
    text_other(1)
    image_relay(0)
    text_own(1)
    image_terms(2)
    image_relay(1)
    image_terms(3)
    image_relay(2)
    image_sums(0)
    text_sums(0)
    image_sums(1)
    image_relay(3)
    image_sums(2)
    image_sums(3)
    text_sums(1)

    for k in (1, 7, 2, 6):
        zz = (z + k) % 8
        for cc in (0, 1):
            got(gz.at[zz, cc], gz_r.at[2 * zz + cc])
    got(gz.at[z, o], gz_r.at[2 * z + o])
    for dd in (h * 2 + o, (1 - h) * 2, (1 - h) * 2 + 1):
        got(gf.at[dd], gf_r.at[dd])
    for r in (0, 1):
        t = gz[z, r].astype(F32)
        for k in (1, 7, 2, 6):
            t = t + gz[(z + k) % 8, r].astype(F32)
        gi_out[r * 32 : (r + 1) * 32] = t
    for dd in range(4):
        gt_out[dd * 96 : (dd + 1) * 96] = gf[dd].astype(F32)
    for cp in sends:
        cp.wait_send()


def on_device(images, texts, image_potential, text_potential):
    given = (images, texts.reshape(4, 96, W), image_potential, text_potential)
    dma = pltpu.SemaphoreType.DMA
    vm = pltpu.VMEM
    hbm = pl.BlockSpec(memory_space=pltpu.HBM)
    return pl.pallas_call(
        kernel,
        out_shape=(jax.ShapeDtypeStruct((64, W), F32), jax.ShapeDtypeStruct((384, W), F32)),
        in_specs=[hbm] * 4,
        out_specs=(pl.BlockSpec(memory_space=pltpu.VMEM), pl.BlockSpec(memory_space=pltpu.VMEM)),
        scratch_shapes=[
            vm((4, 128, 4 * W), BF16), vm((2, 4, 96, 4 * W), BF16), vm((4, 128, 768), BF16),
            vm((64,), F32), vm((W,), F32), vm((4, 8, 128), F32), vm((4, 8, 128), F32), vm((4, 8, 768), F32),
            vm((2, 512, 4 * W), F32), vm((4, 6, 16, 4 * W), BF16), vm((4, 6, 16, 4 * W), BF16), vm((4, 32, 4 * W), BF16),
            vm((8, 2, 32, W), BF16), vm((4, 96, W), BF16),
            vm((2, 16, 2 * W), BF16), vm((2, 32, 2 * W), BF16),
            vm((2, 384, 2 * W), F32), vm((2, 384, 2 * W), BF16), vm((2, 384, 2 * W), BF16),
            vm((2, 3, 96, 2 * W), BF16), vm((2, 3, 96, 2 * W), BF16), vm((2, 96, 2 * W), BF16),
            dma((4,)), dma((4,)), dma((4,)), dma((8,)), dma((8,)), dma((2,)), dma((2,)), dma((12,)), dma((12,)),
            dma((16,)), dma((16,)), dma((16,)), dma((32,)), dma((16,)), dma((16,)),
            dma((4,)), dma((4,)), dma((4,)), dma((4,)), dma((4,)), dma((4,)),
            dma((24,)), dma((24,)), dma((16,)), dma((16,)), dma((4,)), dma((4,)), dma((2,)), dma((2,)), dma((8,)), dma((8,)), dma((4,)), dma((4,)),
        ],
        compiler_params=pltpu.CompilerParams(
            collective_id=0, has_side_effects=True, vmem_limit_bytes=48 * 1024 * 1024
        ),
        cost_estimate=pl.CostEstimate(flops=3623878656, bytes_accessed=2000000, transcendentals=393216),
    )(*(pltpu.with_memory_space_constraint(v, pltpu.HBM) for v in given))


def solution(mesh):
    placed = (
        P(("row", "col"), "depth"),
        P(("row", "col"), "depth"),
        P(("row", "col")),
        P(("row", "col")),
    )
    return jax.shard_map(
        on_device,
        mesh=mesh,
        in_specs=placed,
        out_specs=(P(("row", "col"), "depth"), P(("row", "col"), "depth")),
        check_vma=False,
    )
```

```python
import jax
import jax.numpy as jnp
from jax import lax
from jax.experimental import pallas as pl
from jax.experimental.pallas import tpu as pltpu
from jax.sharding import PartitionSpec as P

INV_TEMP = 0.4
LOSS_SCALE = 16.0
MESH = pl.DeviceIdType.MESH
F32, BF16 = jnp.float32, jnp.bfloat16
ZORDER = (1, 7, 2, 6, 4)
RING = (1, 3, 2)
ORDER = (0, 1, 3, 2)
DIRECT = (4,)
PAIRS = ((0, 4), (1, 5), (7, 3), (2, 6))
W = 384


def dev(x, y, z, c):
    return (y, x * 4 + z % 4, (z // 4) * 2 + c)


def cols(q, n=W):
    return pl.ds(pl.multiple_of(q * W, W), n)


def kernel(
    img_in, txt_in, ip_in, tp_in, gi_out, gt_out,
    img, txt, plan, ipv, tpv, ap, aps, tp,
    gi_own, gi_send, gi_recv, gz_send, gz, gf, gq_recv, gr_recv,
    gt_own, gx_send, gx_recv, gy_send, gy_recv, gf_send,
    loc_sem, yn_s, yn_r, ye_s, ye_r, ex_s, ex_r, ch_s, ch_r, iz_s, iz_r, ix_s, ix_r, fw_s, fw_r,
    tp_s, tp_r, ap_s, ap_r, aps_s, aps_r,
    gi_s, gi_r, gz_s, gz_r, gr_s, gr_r, gx_s, gx_r, gy_s, gy_r, gf_s, gf_r,
):
    y = lax.axis_index("row")
    col = lax.axis_index("col")
    d = lax.axis_index("depth")
    x, zl, h, c = col // 4, col % 4, d // 2, d % 2
    z = h * 4 + zl
    o = 1 - c
    q = 2 * h + c
    qp = 2 * (1 - h) + c

    def rc(src, dst, ss, rs, target):
        return pltpu.make_async_remote_copy(
            src_ref=src, dst_ref=dst, send_sem=ss, recv_sem=rs, device_id=target, device_id_type=MESH
        )

    me_o = dev(x, y, z, o)

    def got(dst, rs):
        rc(dst, dst, yn_s.at[0], rs, me_o).wait_recv()

    bar = pltpu.get_barrier_semaphore()
    partners = [me_o]
    partners += [dev((x + k) % 4, y, z, c) for k in RING]
    partners += [dev(x, (y + k) % 4, z, c) for k in RING]
    partners += [dev(x, y, (z + k) % 8, cc) for k in ZORDER for cc in (0, 1)]
    partners += [dev(x, y, (z + k) % 8, c) for k in (3, 5)]
    for p in partners:
        pl.semaphore_signal(bar, inc=1, device_id=p, device_id_type=MESH)

    lp = [pltpu.make_async_copy(ip_in, ipv, loc_sem.at[2]), pltpu.make_async_copy(tp_in, tpv, loc_sem.at[3])]
    for cp in lp:
        cp.start()
    for cp in lp:
        cp.wait()
    lane = lax.broadcasted_iota(jnp.int32, (8, 128), 1)
    v = ipv[...].reshape(1, 64)
    v = jnp.broadcast_to(jnp.concatenate([v, v], axis=1), (8, 128))
    v = pltpu.roll(v, ((zl + 4 - c) % 4) * 32, 1)
    aps[x] = jnp.where(lane // 32 == zl, v, 0.0)
    lane = lax.broadcasted_iota(jnp.int32, (8, W), 1)
    v = jnp.broadcast_to(tpv[...].reshape(1, W), (8, W))
    for s in (0, 1):
        t = pltpu.roll(v, (y * 96 + 2 * W - h * 192 - s * 96) % W, 1)
        tp[y, :, s * W : (s + 1) * W] = jnp.where(lane // 96 == y, t, 0.0)
    pl.semaphore_wait(bar, len(partners))

    sends = []

    def go(cp):
        cp.start()
        sends.append(cp)

    def text_piece(yy, qq, s):
        return txt.at[s, yy, :, cols(qq)]

    mine = txt_in.at[pl.ds(h * 2, 2)]
    rows_here = pl.ds(pl.multiple_of(x * 32, 32), 32)
    mine = txt_in.at[pl.ds(h * 2, 2)]

    def send_images(k):
        for r in (0, 1):
            go(rc(img_in.at[pl.ds(r * 32, 32)], img.at[zl, rows_here, cols(q)], iz_s.at[2 * min(k, 8 - k) + r + (8 if k > 4 else 0)],
                  iz_r.at[2 * z + c], dev(x, y, (z + k) % 8, r)))

    def send_texts():
        for k in RING:
            go(rc(mine, txt.at[:, y, :, cols(q)], yn_s.at[k], yn_r.at[y], dev(x, (y + k) % 4, z, c)))

    def swap_texts(s):
        go(rc(txt_in.at[(1 - h) * 2 + s], text_piece(y, q, s), ex_s.at[s], ex_r.at[s], dev(x, y, (z + 4) % 8, c)))

    go(rc(img_in.at[pl.ds(pl.multiple_of(o * 32, 32), 32)], img.at[zl, rows_here, cols(q)], iz_s.at[0],
          iz_r.at[2 * z + c], me_o))
    send_images(1)
    send_images(7)
    swap_texts(0)
    send_texts()
    send_images(2)
    send_images(6)
    swap_texts(1)
    loc_i = pltpu.make_async_copy(
        img_in.at[pl.ds(pl.multiple_of(c * 32, 32), 32)], img.at[zl, rows_here, cols(q)], loc_sem.at[1])
    loc_i.start()
    loc_t = pltpu.make_async_copy(mine, txt.at[:, y, :, cols(q)], loc_sem.at[0])
    loc_t.start()
    go(rc(mine, txt.at[:, y, :, cols(q)], ch_s.at[0], ch_r.at[y], me_o))
    for k in RING:
        go(rc(tp.at[y], tp.at[y], tp_s.at[k], tp_r.at[y], dev(x, (y + k) % 4, z, c)))
        go(rc(aps.at[x], ap.at[zl], ap_s.at[k], ap_r.at[zl], dev(x, y, h * 4 + (zl + k) % 4, c)))
    loc_i.wait()

    def piece(xx, zz, start=0, n=32):
        return img.at[zz % 4, pl.ds(pl.multiple_of(xx * 32 + start, 16), n), cols(2 * (zz // 4), 2 * W)]

    def pass_on(k):
        zz = (z + k) % 8
        for e, kx in ((0, 1), (1, 3)):
            back = (x + 4 - kx) % 4
            got(piece(back, zz), ix_r.at[8 * back + zz])
            if k in DIRECT:
                continue
            half = piece(back, zz, 16 * e, 16)
            go(rc(half, half, fw_s.at[2 * k + e], fw_r.at[2 * zz + e], dev((x + kx) % 4, y, z, c)))

    def along_x(k):
        zz = (z + k) % 8
        if k == 0:
            got(img.at[zl, rows_here, cols(2 * h + o)], iz_r.at[2 * z + o])
        elif k in (3, 5):
            got(piece(x, zz), iz_r.at[2 * zz])
        elif k == 4:
            for e in (0, 1):
                got(piece(x, zz, 16 * e, 16), iz_r.at[2 * zz + e])
        else:
            for cc in (0, 1):
                got(img.at[zz % 4, rows_here, cols(2 * (zz // 4) + cc)], iz_r.at[2 * zz + cc])
        if k in (2, 6):
            e, step = (1, 7) if k == 2 else (0, 1)
            p = piece(x, zz)
            go(rc(p, p, iz_s.at[6 + 2 * e], iz_r.at[2 * zz], dev(x, y, (z + step) % 8, c)))
            p = piece(x, zz, 16 * e, 16)
            go(rc(p, p, iz_s.at[7 + 2 * e], iz_r.at[2 * zz + e], dev(x, y, (z + 2 * step) % 8, c)))
        for e, kx in ((0, 1), (1, 3)):
            go(rc(piece(x, zz), piece(x, zz), ix_s.at[2 * k + e], ix_r.at[8 * x + zz], dev((x + kx) % 4, y, z, c)))
        if k in DIRECT:
            for e in (0, 1):
                p = piece(x, zz, 16 * e, 16)
                go(rc(p, p, fw_s.at[2 * k + e], fw_r.at[2 * zz + e], dev((x + 2) % 4, y, z, c)))

    def forward_swapped(s):
        p = text_piece(y, qp, s)
        got(p, ex_r.at[s])
        for ky in RING:
            go(rc(p, p, ye_s.at[2 * ky + s], ye_r.at[2 * y + s], dev(x, (y + ky) % 4, z, c)))
        go(rc(p, p, ch_s.at[4 + s], ch_r.at[4 + 2 * y + s], me_o))

    def to_other_core(ky):
        yy = (y + ky) % 4
        p = txt.at[:, yy, :, cols(q)]
        got(p, yn_r.at[yy])
        go(rc(p, p, ch_s.at[ky], ch_r.at[yy], me_o))

    def swapped_to_other_core(s):
        for ky in RING:
            yy = (y + ky) % 4
            p = text_piece(yy, qp, s)
            got(p, ye_r.at[2 * yy + s])
            go(rc(p, p, ch_s.at[4 + 2 * ky + s], ch_r.at[4 + 2 * yy + s], me_o))

    def potentials(_):
        asum = aps[x]
        for k in RING:
            zz = (zl + k) % 4
            got(ap.at[zz], ap_r.at[zz])
            asum = asum + ap[zz]
        ap[zl] = asum
        for kx in RING:
            go(rc(ap.at[zl], aps.at[x], aps_s.at[kx], aps_r.at[x], dev((x + kx) % 4, y, z, c)))

    along_x(0)
    along_x(1)
    along_x(7)
    pass_on(0)
    forward_swapped(0)
    along_x(2)
    along_x(6)
    potentials(0)
    pass_on(1)
    pass_on(7)
    forward_swapped(1)
    along_x(3)
    along_x(5)
    pass_on(2)
    pass_on(6)
    along_x(4)
    to_other_core(1)
    to_other_core(3)
    to_other_core(2)
    pass_on(3)
    pass_on(5)
    pass_on(4)
    swapped_to_other_core(0)
    swapped_to_other_core(1)

    loc_t.wait()
    tsum = tp[y]
    for ky in RING:
        yy = (y + ky) % 4
        got(tp.at[yy], tp_r.at[yy])
        tsum = tsum + tp[yy]
    b = tsum[0:1]
    a_of = {0: jnp.broadcast_to(ap[zl][0:1], (128, 128)).T}
    for kx in RING:
        xx = (x + kx) % 4
        got(aps.at[xx], aps_r.at[xx])
        a_of[kx] = jnp.broadcast_to(aps[xx][0:1], (128, 128)).T
    for kx in (0,) + RING:
        gi_own[0, pl.ds(pl.multiple_of(((x + kx) % 4) * 128, 128), 128), 0:128] = a_of[kx]
    for ky in (0,) + RING:
        yy = (y + ky) % 4
        got(txt.at[:, yy, :, cols(2 * h + o)], ch_r.at[yy])
        for s in (0, 1):
            got(text_piece(yy, 2 * (1 - h) + o, s), ch_r.at[4 + 2 * yy + s])

    texts = txt[...].reshape(768, 4 * W)

    def scores(half):
        if half == 0:
            for zz in range(8):
                for e in (0, 1):
                    got(piece((x + 2) % 4, zz, 16 * e, 16), fw_r.at[2 * zz + e])
        a = jnp.concatenate(
            [gi_own[0, pl.ds(xx * 128 + zz * 32, 32), 0:128] for zz in (2 * half, 2 * half + 1) for xx in range(4)], axis=0)
        i = img[2 * half : 2 * half + 2].reshape(256, 4 * W)
        t = lax.dot_general(i, texts, (((1,), (1,)), ((), ())), preferred_element_type=F32)
        p = jnp.exp(t * INV_TEMP + jnp.concatenate([a] * 6, axis=1) + b).astype(BF16)
        plan[2 * half : 2 * half + 2] = p.reshape(2, 128, 768)

    def own_rows(j, k, e, n=16):
        return pl.ds(pl.multiple_of(j * 128 + ((x + k) % 4) * 32 + 16 * e, 16), n)

    def image_send(j, slot, kx):
        go(rc(gi_send.at[j, slot], gi_recv.at[j, slot], gi_s.at[6 * j + slot], gi_r.at[6 * j + slot],
              dev((x + kx) % 4, y, z, c)))

    def image_terms(j):
        zj = (zl + ORDER[j]) % 4
        gi_own[1, pl.ds(j * 128, 128)] = jnp.dot(plan[zj], texts, preferred_element_type=F32) * (-LOSS_SCALE / 24576)
        for slot, (k, e, kx) in enumerate(((2, 0, 1), (2, 1, 3), (1, 1, 1), (3, 0, 3))):
            gi_send[j, slot] = gi_own[1, own_rows(j, k, e)].astype(BF16)
            image_send(j, slot, kx)

    def image_relay(j):
        for slot, (k, e) in enumerate(((1, 0), (3, 1))):
            got(gi_recv.at[j, slot], gi_r.at[6 * j + slot])
            gi_send[j, 4 + slot] = (gi_own[1, own_rows(j, k, e)] + gi_recv[j, slot].astype(F32)).astype(BF16)
            image_send(j, 4 + slot, k)

    def text_terms(half, cc):
        p = plan[:, :, pl.ds(pl.multiple_of(half * W, W), W)].reshape(512, W)
        i = img[:, :, cc].reshape(512, 2 * W)
        return lax.dot_general(p, i, (((0,), (0,)), ((), ())), preferred_element_type=F32) * (-LOSS_SCALE / 4096)

    wide = [cols(2 * (1 - h), 2 * W), cols(2 * h, 2 * W)]

    def text_other(j):
        gx_send[j] = text_terms(o, wide[j]).astype(BF16)
        go(rc(gx_send.at[j], gx_recv.at[j], gx_s.at[j], gx_r.at[j], me_o))

    def text_own(j):
        gt_own[j] = text_terms(c, wide[j])
        got(gx_recv.at[j], gx_r.at[j])
        for i, k in enumerate(RING):
            yy = (y + k) % 4
            rows = pl.ds(pl.multiple_of(yy * 96, 96), 96)
            gy_send[j, i] = (gt_own[j, rows] + gx_recv[j, rows].astype(F32)).astype(BF16)
            go(rc(gy_send.at[j, i], gy_recv.at[j, k - 1], gy_s.at[4 * j + k], gy_r.at[4 * j + k], dev(x, yy, z, c)))

    def image_sums(j):
        for slot in (2, 3, 4, 5):
            got(gi_recv.at[j, slot], gi_r.at[6 * j + slot])
        for e, slots in ((0, (3, 4)), (1, (2, 5))):
            t = gi_own[1, own_rows(j, 0, e)]
            for slot in slots:
                t = t + gi_recv[j, slot].astype(F32)
            if j < 3:
                gz_send[j, 16 * e : 16 * e + 16] = t.astype(BF16)
            else:
                gi_own[0, 16 * e : 16 * e + 16] = t
        for dz in PAIRS[j]:
            zz = (z + dz) % 8
            both = cols(2 * (zz // 4), 2 * W)
            if dz == 4:
                for e, step in ((0, 2), (1, 6)):
                    go(rc(gz_send.at[j, pl.ds(16 * e, 16), both], gq_recv.at[e], gr_s.at[e], gr_r.at[e],
                          dev(x, y, (z + step) % 8, c)))
            elif dz in (3, 5):
                e, step = (0, 1) if dz == 3 else (1, 7)
                go(rc(gz_send.at[j, :, both], gr_recv.at[e], gr_s.at[2 + e], gr_r.at[2 + e],
                      dev(x, y, (z + step) % 8, c)))
            elif dz == 0:
                go(rc(gz_send.at[0, :, cols(2 * h + o)], gz.at[z, c], gz_s.at[0], gz_r.at[2 * z + c], me_o))
                gz[z, c] = gz_send[0, :, cols(q)]
            else:
                if dz in (2, 6):
                    e = 0 if dz == 2 else 1
                    got(gq_recv.at[e], gr_r.at[e])
                    got(gr_recv.at[e], gr_r.at[2 + e])
                    for g in (0, 1):
                        t = gi_own[0, 16 * g : 16 * g + 16, both] + gr_recv[e, 16 * g : 16 * g + 16].astype(F32)
                        if g == e:
                            t = t + gq_recv[e].astype(F32)
                        gz_send[j, 16 * g : 16 * g + 16, both] = t.astype(BF16)
                for cc in (0, 1):
                    go(rc(gz_send.at[j, :, cols(2 * (zz // 4) + cc)], gz.at[z, c], gz_s.at[2 * dz + cc],
                          gz_r.at[2 * z + c], dev(x, y, zz, cc)))

    def text_sums(j):
        mine_y = pl.ds(pl.multiple_of(y * 96, 96), 96)
        t = gt_own[j, mine_y] + gx_recv[j, mine_y].astype(F32)
        for k in RING:
            got(gy_recv.at[j, k - 1], gy_r.at[4 * j + k])
            t = t + gy_recv[j, k - 1].astype(F32)
        gf_send[j] = t.astype(BF16)
        part = gf.at[h * 2 + c]
        if j == 0:
            for cc in (0, 1):
                go(rc(gf_send.at[0, :, pl.ds(cc * W, W)], part, gf_s.at[cc], gf_r.at[h * 2 + c], dev(x, y, (z + 4) % 8, cc)))
        else:
            go(rc(gf_send.at[1, :, cols(o)], part, gf_s.at[2], gf_r.at[h * 2 + c], me_o))
            gf[h * 2 + c] = gf_send[1, :, cols(c)]

    scores(0)
    scores(1)
    text_other(0)
    image_terms(0)
    text_own(0)
    image_terms(1)
    text_other(1)
    image_relay(0)
    text_own(1)
    image_terms(2)
    image_relay(1)
    image_terms(3)
    image_relay(2)
    image_sums(0)
    text_sums(0)
    image_sums(1)
    image_relay(3)
    image_sums(2)
    image_sums(3)
    text_sums(1)

    for k in (1, 7, 2, 6):
        zz = (z + k) % 8
        for cc in (0, 1):
            got(gz.at[zz, cc], gz_r.at[2 * zz + cc])
    got(gz.at[z, o], gz_r.at[2 * z + o])
    for dd in (h * 2 + o, (1 - h) * 2, (1 - h) * 2 + 1):
        got(gf.at[dd], gf_r.at[dd])
    for r in (0, 1):
        t = gz[z, r].astype(F32)
        for k in (1, 7, 2, 6):
            t = t + gz[(z + k) % 8, r].astype(F32)
        gi_out[r * 32 : (r + 1) * 32] = t
    for dd in range(4):
        gt_out[dd * 96 : (dd + 1) * 96] = gf[dd].astype(F32)
    for cp in sends:
        cp.wait_send()


def on_device(images, texts, image_potential, text_potential):
    given = (images, texts.reshape(4, 96, W), image_potential, text_potential)
    dma = pltpu.SemaphoreType.DMA
    vm = pltpu.VMEM
    hbm = pl.BlockSpec(memory_space=pltpu.HBM)
    return pl.pallas_call(
        kernel,
        out_shape=(jax.ShapeDtypeStruct((64, W), F32), jax.ShapeDtypeStruct((384, W), F32)),
        in_specs=[hbm] * 4,
        out_specs=(pl.BlockSpec(memory_space=pltpu.VMEM), pl.BlockSpec(memory_space=pltpu.VMEM)),
        scratch_shapes=[
            vm((4, 128, 4 * W), BF16), vm((2, 4, 96, 4 * W), BF16), vm((4, 128, 768), BF16),
            vm((64,), F32), vm((W,), F32), vm((4, 8, 128), F32), vm((4, 8, 128), F32), vm((4, 8, 768), F32),
            vm((2, 512, 4 * W), F32), vm((4, 6, 16, 4 * W), BF16), vm((4, 6, 16, 4 * W), BF16), vm((4, 32, 4 * W), BF16),
            vm((8, 2, 32, W), BF16), vm((4, 96, W), BF16),
            vm((2, 16, 2 * W), BF16), vm((2, 32, 2 * W), BF16),
            vm((2, 384, 2 * W), F32), vm((2, 384, 2 * W), BF16), vm((2, 384, 2 * W), BF16),
            vm((2, 3, 96, 2 * W), BF16), vm((2, 3, 96, 2 * W), BF16), vm((2, 96, 2 * W), BF16),
            dma((4,)), dma((4,)), dma((4,)), dma((8,)), dma((8,)), dma((2,)), dma((2,)), dma((12,)), dma((12,)),
            dma((16,)), dma((16,)), dma((16,)), dma((32,)), dma((16,)), dma((16,)),
            dma((4,)), dma((4,)), dma((4,)), dma((4,)), dma((4,)), dma((4,)),
            dma((24,)), dma((24,)), dma((16,)), dma((16,)), dma((4,)), dma((4,)), dma((2,)), dma((2,)), dma((8,)), dma((8,)), dma((4,)), dma((4,)),
        ],
        compiler_params=pltpu.CompilerParams(
            collective_id=0, has_side_effects=True, vmem_limit_bytes=48 * 1024 * 1024
        ),
        cost_estimate=pl.CostEstimate(flops=3623878656, bytes_accessed=2000000, transcendentals=393216),
    )(*(pltpu.with_memory_space_constraint(v, pltpu.HBM) for v in given))


def solution(mesh):
    placed = (
        P(("row", "col"), "depth"),
        P(("row", "col"), "depth"),
        P(("row", "col")),
        P(("row", "col")),
    )
    return jax.shard_map(
        on_device,
        mesh=mesh,
        in_specs=placed,
        out_specs=(P(("row", "col"), "depth"), P(("row", "col"), "depth")),
        check_vma=False,
    )
```

```python
import jax
import jax.numpy as jnp
from jax import lax
from jax.experimental import pallas as pl
from jax.experimental.pallas import tpu as pltpu
from jax.sharding import PartitionSpec as P

INV_TEMP = 0.4
LOSS_SCALE = 16.0
MESH = pl.DeviceIdType.MESH
F32, BF16 = jnp.float32, jnp.bfloat16
ZORDER = (1, 7, 2, 6, 4)
RING = (1, 3, 2)
ORDER = (0, 1, 3, 2)
DIRECT = (4,)
PAIRS = ((0, 4), (1, 5), (7, 3), (2, 6))
W = 384


def dev(x, y, z, c):
    return (y, x * 4 + z % 4, (z // 4) * 2 + c)


def cols(q, n=W):
    return pl.ds(pl.multiple_of(q * W, W), n)


def kernel(
    img_in, txt_in, ip_in, tp_in, gi_out, gt_out,
    img, txt, plan, ipv, tpv, ap, aps, tp,
    gi_own, gi_send, gi_recv, gz_send, gz, gf, gq_recv, gr_recv,
    gt_own, gx_send, gx_recv, gy_send, gy_recv, gf_send,
    loc_sem, yn_s, yn_r, ye_s, ye_r, ex_s, ex_r, ch_s, ch_r, iz_s, iz_r, ix_s, ix_r, fw_s, fw_r,
    tp_s, tp_r, ap_s, ap_r, aps_s, aps_r,
    gi_s, gi_r, gz_s, gz_r, gr_s, gr_r, gx_s, gx_r, gy_s, gy_r, gf_s, gf_r,
):
    y = lax.axis_index("row")
    col = lax.axis_index("col")
    d = lax.axis_index("depth")
    x, zl, h, c = col // 4, col % 4, d // 2, d % 2
    z = h * 4 + zl
    o = 1 - c
    q = 2 * h + c
    qp = 2 * (1 - h) + c

    def rc(src, dst, ss, rs, target):
        return pltpu.make_async_remote_copy(
            src_ref=src, dst_ref=dst, send_sem=ss, recv_sem=rs, device_id=target, device_id_type=MESH
        )

    me_o = dev(x, y, z, o)

    def got(dst, rs):
        rc(dst, dst, yn_s.at[0], rs, me_o).wait_recv()

    bar = pltpu.get_barrier_semaphore()
    partners = [me_o]
    partners += [dev((x + k) % 4, y, z, c) for k in RING]
    partners += [dev(x, (y + k) % 4, z, c) for k in RING]
    partners += [dev(x, y, (z + k) % 8, cc) for k in ZORDER for cc in (0, 1)]
    partners += [dev(x, y, (z + k) % 8, c) for k in (3, 5)]
    for p in partners:
        pl.semaphore_signal(bar, inc=1, device_id=p, device_id_type=MESH)

    lp = [pltpu.make_async_copy(ip_in, ipv, loc_sem.at[2]), pltpu.make_async_copy(tp_in, tpv, loc_sem.at[3])]
    for cp in lp:
        cp.start()
    for cp in lp:
        cp.wait()
    lane = lax.broadcasted_iota(jnp.int32, (8, 128), 1)
    v = ipv[...].reshape(1, 64)
    v = jnp.broadcast_to(jnp.concatenate([v, v], axis=1), (8, 128))
    v = pltpu.roll(v, ((zl + 4 - c) % 4) * 32, 1)
    aps[x] = jnp.where(lane // 32 == zl, v, 0.0)
    lane = lax.broadcasted_iota(jnp.int32, (8, W), 1)
    v = jnp.broadcast_to(tpv[...].reshape(1, W), (8, W))
    for s in (0, 1):
        t = pltpu.roll(v, (y * 96 + 2 * W - h * 192 - s * 96) % W, 1)
        tp[y, :, s * W : (s + 1) * W] = jnp.where(lane // 96 == y, t, 0.0)
    pl.semaphore_wait(bar, len(partners))

    sends = []

    def go(cp):
        cp.start()
        sends.append(cp)

    def text_piece(yy, qq, s):
        return txt.at[s, yy, :, cols(qq)]

    mine = txt_in.at[pl.ds(h * 2, 2)]
    rows_here = pl.ds(pl.multiple_of(x * 32, 32), 32)
    mine = txt_in.at[pl.ds(h * 2, 2)]

    def send_images(k):
        for r in (0, 1):
            go(rc(img_in.at[pl.ds(r * 32, 32)], img.at[zl, rows_here, cols(q)], iz_s.at[2 * min(k, 8 - k) + r + (8 if k > 4 else 0)],
                  iz_r.at[2 * z + c], dev(x, y, (z + k) % 8, r)))

    def send_texts():
        for k in RING:
            go(rc(mine, txt.at[:, y, :, cols(q)], yn_s.at[k], yn_r.at[y], dev(x, (y + k) % 4, z, c)))

    def swap_texts(s):
        go(rc(txt_in.at[(1 - h) * 2 + s], text_piece(y, q, s), ex_s.at[s], ex_r.at[s], dev(x, y, (z + 4) % 8, c)))

    go(rc(img_in.at[pl.ds(pl.multiple_of(o * 32, 32), 32)], img.at[zl, rows_here, cols(q)], iz_s.at[0],
          iz_r.at[2 * z + c], me_o))
    send_images(1)
    send_images(7)
    swap_texts(0)
    send_texts()
    send_images(2)
    send_images(6)
    swap_texts(1)
    loc_i = pltpu.make_async_copy(
        img_in.at[pl.ds(pl.multiple_of(c * 32, 32), 32)], img.at[zl, rows_here, cols(q)], loc_sem.at[1])
    loc_i.start()
    loc_t = pltpu.make_async_copy(mine, txt.at[:, y, :, cols(q)], loc_sem.at[0])
    loc_t.start()
    go(rc(mine, txt.at[:, y, :, cols(q)], ch_s.at[0], ch_r.at[y], me_o))
    for k in RING:
        go(rc(tp.at[y], tp.at[y], tp_s.at[k], tp_r.at[y], dev(x, (y + k) % 4, z, c)))
        go(rc(aps.at[x], ap.at[zl], ap_s.at[k], ap_r.at[zl], dev(x, y, h * 4 + (zl + k) % 4, c)))
    loc_i.wait()

    def piece(xx, zz, start=0, n=32):
        return img.at[zz % 4, pl.ds(pl.multiple_of(xx * 32 + start, 16), n), cols(2 * (zz // 4), 2 * W)]

    def pass_on(k):
        zz = (z + k) % 8
        for e, kx in ((0, 1), (1, 3)):
            back = (x + 4 - kx) % 4
            got(piece(back, zz), ix_r.at[8 * back + zz])
            if k in DIRECT:
                continue
            half = piece(back, zz, 16 * e, 16)
            go(rc(half, half, fw_s.at[2 * k + e], fw_r.at[2 * zz + e], dev((x + kx) % 4, y, z, c)))

    def along_x(k):
        zz = (z + k) % 8
        if k == 0:
            got(img.at[zl, rows_here, cols(2 * h + o)], iz_r.at[2 * z + o])
        elif k in (3, 5):
            got(piece(x, zz), iz_r.at[2 * zz])
        elif k == 4:
            for e in (0, 1):
                got(piece(x, zz, 16 * e, 16), iz_r.at[2 * zz + e])
        else:
            for cc in (0, 1):
                got(img.at[zz % 4, rows_here, cols(2 * (zz // 4) + cc)], iz_r.at[2 * zz + cc])
        if k in (2, 6):
            e, step = (1, 7) if k == 2 else (0, 1)
            p = piece(x, zz)
            go(rc(p, p, iz_s.at[6 + 2 * e], iz_r.at[2 * zz], dev(x, y, (z + step) % 8, c)))
            p = piece(x, zz, 16 * e, 16)
            go(rc(p, p, iz_s.at[7 + 2 * e], iz_r.at[2 * zz + e], dev(x, y, (z + 2 * step) % 8, c)))
        for e, kx in ((0, 1), (1, 3)):
            go(rc(piece(x, zz), piece(x, zz), ix_s.at[2 * k + e], ix_r.at[8 * x + zz], dev((x + kx) % 4, y, z, c)))
        if k in DIRECT:
            for e in (0, 1):
                p = piece(x, zz, 16 * e, 16)
                go(rc(p, p, fw_s.at[2 * k + e], fw_r.at[2 * zz + e], dev((x + 2) % 4, y, z, c)))

    def forward_swapped(s):
        p = text_piece(y, qp, s)
        got(p, ex_r.at[s])
        for ky in RING:
            go(rc(p, p, ye_s.at[2 * ky + s], ye_r.at[2 * y + s], dev(x, (y + ky) % 4, z, c)))
        go(rc(p, p, ch_s.at[4 + s], ch_r.at[4 + 2 * y + s], me_o))

    def to_other_core(ky):
        yy = (y + ky) % 4
        p = txt.at[:, yy, :, cols(q)]
        got(p, yn_r.at[yy])
        go(rc(p, p, ch_s.at[ky], ch_r.at[yy], me_o))

    def swapped_to_other_core(s):
        for ky in RING:
            yy = (y + ky) % 4
            p = text_piece(yy, qp, s)
            got(p, ye_r.at[2 * yy + s])
            go(rc(p, p, ch_s.at[4 + 2 * ky + s], ch_r.at[4 + 2 * yy + s], me_o))

    def potentials(_):
        asum = aps[x]
        for k in RING:
            zz = (zl + k) % 4
            got(ap.at[zz], ap_r.at[zz])
            asum = asum + ap[zz]
        ap[zl] = asum
        for kx in RING:
            go(rc(ap.at[zl], aps.at[x], aps_s.at[kx], aps_r.at[x], dev((x + kx) % 4, y, z, c)))

    along_x(0)
    along_x(1)
    along_x(7)
    pass_on(0)
    forward_swapped(0)
    along_x(2)
    along_x(6)
    potentials(0)
    pass_on(1)
    pass_on(7)
    forward_swapped(1)
    along_x(3)
    along_x(5)
    pass_on(2)
    pass_on(6)
    along_x(4)
    to_other_core(1)
    to_other_core(3)
    to_other_core(2)
    pass_on(3)
    pass_on(5)
    pass_on(4)
    swapped_to_other_core(0)
    swapped_to_other_core(1)

    loc_t.wait()
    tsum = tp[y]
    for ky in RING:
        yy = (y + ky) % 4
        got(tp.at[yy], tp_r.at[yy])
        tsum = tsum + tp[yy]
    b = tsum[0:1]
    a_of = {0: jnp.broadcast_to(ap[zl][0:1], (128, 128)).T}
    for kx in RING:
        xx = (x + kx) % 4
        got(aps.at[xx], aps_r.at[xx])
        a_of[kx] = jnp.broadcast_to(aps[xx][0:1], (128, 128)).T
    for kx in (0,) + RING:
        gi_own[0, pl.ds(pl.multiple_of(((x + kx) % 4) * 128, 128), 128), 0:128] = a_of[kx]
    for ky in (0,) + RING:
        yy = (y + ky) % 4
        got(txt.at[:, yy, :, cols(2 * h + o)], ch_r.at[yy])
        for s in (0, 1):
            got(text_piece(yy, 2 * (1 - h) + o, s), ch_r.at[4 + 2 * yy + s])

    texts = txt[...].reshape(768, 4 * W)

    def scores(half):
        if half == 0:
            for zz in range(8):
                for e in (0, 1):
                    got(piece((x + 2) % 4, zz, 16 * e, 16), fw_r.at[2 * zz + e])
        a = jnp.concatenate(
            [gi_own[0, pl.ds(xx * 128 + zz * 32, 32), 0:128] for zz in (2 * half, 2 * half + 1) for xx in range(4)], axis=0)
        i = img[2 * half : 2 * half + 2].reshape(256, 4 * W)
        t = lax.dot_general(i, texts, (((1,), (1,)), ((), ())), preferred_element_type=F32)
        p = jnp.exp(t * INV_TEMP + jnp.concatenate([a] * 6, axis=1) + b).astype(BF16)
        plan[2 * half : 2 * half + 2] = p.reshape(2, 128, 768)

    def own_rows(j, k, e, n=16):
        return pl.ds(pl.multiple_of(j * 128 + ((x + k) % 4) * 32 + 16 * e, 16), n)

    def image_send(j, slot, kx):
        go(rc(gi_send.at[j, slot], gi_recv.at[j, slot], gi_s.at[6 * j + slot], gi_r.at[6 * j + slot],
              dev((x + kx) % 4, y, z, c)))

    def image_terms(j):
        zj = (zl + ORDER[j]) % 4
        gi_own[1, pl.ds(j * 128, 128)] = jnp.dot(plan[zj], texts, preferred_element_type=F32) * (-LOSS_SCALE / 24576)
        for slot, (k, e, kx) in enumerate(((2, 0, 1), (2, 1, 3), (1, 1, 1), (3, 0, 3))):
            gi_send[j, slot] = gi_own[1, own_rows(j, k, e)].astype(BF16)
            image_send(j, slot, kx)

    def image_relay(j):
        for slot, (k, e) in enumerate(((1, 0), (3, 1))):
            got(gi_recv.at[j, slot], gi_r.at[6 * j + slot])
            gi_send[j, 4 + slot] = (gi_own[1, own_rows(j, k, e)] + gi_recv[j, slot].astype(F32)).astype(BF16)
            image_send(j, 4 + slot, k)

    def text_terms(half, cc):
        p = plan[:, :, pl.ds(pl.multiple_of(half * W, W), W)].reshape(512, W)
        i = img[:, :, cc].reshape(512, 2 * W)
        return lax.dot_general(p, i, (((0,), (0,)), ((), ())), preferred_element_type=F32) * (-LOSS_SCALE / 4096)

    wide = [cols(2 * (1 - h), 2 * W), cols(2 * h, 2 * W)]

    def text_other(j):
        gx_send[j] = text_terms(o, wide[j]).astype(BF16)
        go(rc(gx_send.at[j], gx_recv.at[j], gx_s.at[j], gx_r.at[j], me_o))

    def text_own(j):
        gt_own[j] = text_terms(c, wide[j])
        got(gx_recv.at[j], gx_r.at[j])
        for i, k in enumerate(RING):
            yy = (y + k) % 4
            rows = pl.ds(pl.multiple_of(yy * 96, 96), 96)
            gy_send[j, i] = (gt_own[j, rows] + gx_recv[j, rows].astype(F32)).astype(BF16)
            go(rc(gy_send.at[j, i], gy_recv.at[j, k - 1], gy_s.at[4 * j + k], gy_r.at[4 * j + k], dev(x, yy, z, c)))

    def image_sums(j):
        for slot in (2, 3, 4, 5):
            got(gi_recv.at[j, slot], gi_r.at[6 * j + slot])
        for e, slots in ((0, (3, 4)), (1, (2, 5))):
            t = gi_own[1, own_rows(j, 0, e)]
            for slot in slots:
                t = t + gi_recv[j, slot].astype(F32)
            if j < 3:
                gz_send[j, 16 * e : 16 * e + 16] = t.astype(BF16)
            else:
                gi_own[0, 16 * e : 16 * e + 16] = t
        for dz in PAIRS[j]:
            zz = (z + dz) % 8
            both = cols(2 * (zz // 4), 2 * W)
            if dz == 4:
                for e, step in ((0, 2), (1, 6)):
                    go(rc(gz_send.at[j, pl.ds(16 * e, 16), both], gq_recv.at[e], gr_s.at[e], gr_r.at[e],
                          dev(x, y, (z + step) % 8, c)))
            elif dz in (3, 5):
                e, step = (0, 1) if dz == 3 else (1, 7)
                go(rc(gz_send.at[j, :, both], gr_recv.at[e], gr_s.at[2 + e], gr_r.at[2 + e],
                      dev(x, y, (z + step) % 8, c)))
            elif dz == 0:
                go(rc(gz_send.at[0, :, cols(2 * h + o)], gz.at[z, c], gz_s.at[0], gz_r.at[2 * z + c], me_o))
                gz[z, c] = gz_send[0, :, cols(q)]
            else:
                if dz in (2, 6):
                    e = 0 if dz == 2 else 1
                    got(gq_recv.at[e], gr_r.at[e])
                    got(gr_recv.at[e], gr_r.at[2 + e])
                    for g in (0, 1):
                        t = gi_own[0, 16 * g : 16 * g + 16, both] + gr_recv[e, 16 * g : 16 * g + 16].astype(F32)
                        if g == e:
                            t = t + gq_recv[e].astype(F32)
                        gz_send[j, 16 * g : 16 * g + 16, both] = t.astype(BF16)
                for cc in (0, 1):
                    go(rc(gz_send.at[j, :, cols(2 * (zz // 4) + cc)], gz.at[z, c], gz_s.at[2 * dz + cc],
                          gz_r.at[2 * z + c], dev(x, y, zz, cc)))

    def text_sums(j):
        mine_y = pl.ds(pl.multiple_of(y * 96, 96), 96)
        t = gt_own[j, mine_y] + gx_recv[j, mine_y].astype(F32)
        for k in RING:
            got(gy_recv.at[j, k - 1], gy_r.at[4 * j + k])
            t = t + gy_recv[j, k - 1].astype(F32)
        gf_send[j] = t.astype(BF16)
        part = gf.at[h * 2 + c]
        if j == 0:
            for cc in (0, 1):
                go(rc(gf_send.at[0, :, pl.ds(cc * W, W)], part, gf_s.at[cc], gf_r.at[h * 2 + c], dev(x, y, (z + 4) % 8, cc)))
        else:
            go(rc(gf_send.at[1, :, cols(o)], part, gf_s.at[2], gf_r.at[h * 2 + c], me_o))
            gf[h * 2 + c] = gf_send[1, :, cols(c)]

    scores(0)
    scores(1)
    text_other(0)
    image_terms(0)
    text_own(0)
    image_terms(1)
    text_other(1)
    image_relay(0)
    text_own(1)
    image_terms(2)
    image_relay(1)
    image_terms(3)
    image_relay(2)
    image_sums(0)
    text_sums(0)
    image_sums(1)
    image_relay(3)
    image_sums(2)
    image_sums(3)
    text_sums(1)

    for dd in (h * 2 + o, (1 - h) * 2, (1 - h) * 2 + 1):
        got(gf.at[dd], gf_r.at[dd])
    for dd in range(4):
        gt_out[dd * 96 : (dd + 1) * 96] = gf[dd].astype(F32)
    for cp in sends:
        cp.wait_send()
    for k in (1, 7, 2, 6):
        zz = (z + k) % 8
        for cc in (0, 1):
            got(gz.at[zz, cc], gz_r.at[2 * zz + cc])
    got(gz.at[z, o], gz_r.at[2 * z + o])
    for r in (0, 1):
        t = gz[z, r].astype(F32)
        for k in (1, 7, 2, 6):
            t = t + gz[(z + k) % 8, r].astype(F32)
        gi_out[r * 32 : (r + 1) * 32] = t


def on_device(images, texts, image_potential, text_potential):
    given = (images, texts.reshape(4, 96, W), image_potential, text_potential)
    dma = pltpu.SemaphoreType.DMA
    vm = pltpu.VMEM
    hbm = pl.BlockSpec(memory_space=pltpu.HBM)
    return pl.pallas_call(
        kernel,
        out_shape=(jax.ShapeDtypeStruct((64, W), F32), jax.ShapeDtypeStruct((384, W), F32)),
        in_specs=[hbm] * 4,
        out_specs=(pl.BlockSpec(memory_space=pltpu.VMEM), pl.BlockSpec(memory_space=pltpu.VMEM)),
        scratch_shapes=[
            vm((4, 128, 4 * W), BF16), vm((2, 4, 96, 4 * W), BF16), vm((4, 128, 768), BF16),
            vm((64,), F32), vm((W,), F32), vm((4, 8, 128), F32), vm((4, 8, 128), F32), vm((4, 8, 768), F32),
            vm((2, 512, 4 * W), F32), vm((4, 6, 16, 4 * W), BF16), vm((4, 6, 16, 4 * W), BF16), vm((4, 32, 4 * W), BF16),
            vm((8, 2, 32, W), BF16), vm((4, 96, W), BF16),
            vm((2, 16, 2 * W), BF16), vm((2, 32, 2 * W), BF16),
            vm((2, 384, 2 * W), F32), vm((2, 384, 2 * W), BF16), vm((2, 384, 2 * W), BF16),
            vm((2, 3, 96, 2 * W), BF16), vm((2, 3, 96, 2 * W), BF16), vm((2, 96, 2 * W), BF16),
            dma((4,)), dma((4,)), dma((4,)), dma((8,)), dma((8,)), dma((2,)), dma((2,)), dma((12,)), dma((12,)),
            dma((16,)), dma((16,)), dma((16,)), dma((32,)), dma((16,)), dma((16,)),
            dma((4,)), dma((4,)), dma((4,)), dma((4,)), dma((4,)), dma((4,)),
            dma((24,)), dma((24,)), dma((16,)), dma((16,)), dma((4,)), dma((4,)), dma((2,)), dma((2,)), dma((8,)), dma((8,)), dma((4,)), dma((4,)),
        ],
        compiler_params=pltpu.CompilerParams(
            collective_id=0, has_side_effects=True, vmem_limit_bytes=48 * 1024 * 1024
        ),
        cost_estimate=pl.CostEstimate(flops=3623878656, bytes_accessed=2000000, transcendentals=393216),
    )(*(pltpu.with_memory_space_constraint(v, pltpu.HBM) for v in given))


def solution(mesh):
    placed = (
        P(("row", "col"), "depth"),
        P(("row", "col"), "depth"),
        P(("row", "col")),
        P(("row", "col")),
    )
    return jax.shard_map(
        on_device,
        mesh=mesh,
        in_specs=placed,
        out_specs=(P(("row", "col"), "depth"), P(("row", "col"), "depth")),
        check_vma=False,
    )
```
